256 devices in a mesh: replica: 4 (over z_hi), fsdp: 64 (over z_lo, x, y, core).
Axes of the slice: x: 4, y: 4, z: 8 (z_hi: 4, z_lo: 2; z = z_hi * 2 + z_lo), core: 2. Of those that a mesh axis runs over, the one named last changes fastest.
Arguments:
- tokens: bfloat16 [16384, 6144], P(('replica', 'fsdp')), may hold values from -6 to 6
- expert_ids: int32 [16384, 2], P(('replica', 'fsdp')), may hold values from 0 to 7, as said below
- router_weight: bfloat16 [4, 8, 6144], P('replica'), may hold values from -6 to 6
- expert_weights: bfloat16 [4, 3, 6144, 8192], P('replica', None, None, 'fsdp'), may hold values from -6 to 6
- outer_params: float32 [768, 8192], P(None, 'fsdp'), may hold values from -6 to 6
- outer_momentum: float32 [768, 8192], P(None, 'fsdp'), may hold values from -3 to 3
- inner_drift: float32 [4, 768, 8192], P('replica', None, 'fsdp'), may hold values from -3 to 3
- frag_index: int32 [1], replicated, may hold values from 0 to 23
- out_grad: bfloat16 [16384, 6144], P(('replica', 'fsdp')), may hold values from -6 to 6
Outputs:
- expert_out: bfloat16 [16384, 6144], P(('replica', 'fsdp'))
- token_grad: bfloat16 [16384, 6144], P(('replica', 'fsdp'))
- new_params: float32 [768, 8192], P(None, 'fsdp')
- new_momentum: float32 [768, 8192], P(None, 'fsdp')
The draws below stay inside these ranges and needn't reach their ends.
Inputs may be any that keep to these rules, and one draw needn't show every extreme that they name: `expert_ids`: each token names two different experts; in each aligned block of 64 tokens (the tokens of one device) exactly 3 tokens name expert 0.
All inputs are finite; a program needn't handle non-finite values.
Results may differ from the reference program's by a relative error of at most 0.0065.
Values may be sent and summed in bfloat16 or wider, within the bound.
A program may use at most 128 MiB of HBM per device.

```python
import math
from functools import partial
import jax
import jax.numpy as jnp
from jax import lax

D = 6144
FF = 8192
EXPERTS = 8
NFRAG = 24
TOK_DEV = 64
CAP = 3
FR = 768
REPLICAS = 4
TOKENS = 16384
N_REPLICA = 4
N_FSDP = 64


def draw_expert_ids(key, part):
    key = jax.random.fold_in(key, 11)
    blocks = TOKENS // TOK_DEV
    key_perm, key_first, key_shift, key_slot = jax.random.split(key, 4)
    block_keys = jax.random.split(key_perm, blocks)
    orders = jax.vmap(lambda k: jax.random.permutation(k, TOK_DEV))(block_keys)
    chosen = orders < CAP
    first = jax.random.randint(key_first, (blocks, TOK_DEV), 1, EXPERTS)
    shifts = jax.random.randint(key_shift, (blocks, TOK_DEV), 1, EXPERTS - 1)
    second = 1 + (first - 1 + shifts) % (EXPERTS - 1)
    placed = jax.random.randint(key_slot, (blocks, TOK_DEV), 0, 2)
    zeros = jnp.zeros_like(first)
    left = jnp.where(chosen, jnp.where(placed == 0, zeros, first), first)
    right = jnp.where(chosen, jnp.where(placed == 0, first, zeros), second)
    paired = jnp.stack([left, right], axis=-1)
    return paired.reshape(TOKENS, 2).astype(jnp.int32)


def block_levels(own_key, shape, cuts, smallest, top_value):
    gain = 1.0
    for axis_at, parts in cuts:
        steps = jax.random.uniform(jax.random.fold_in(jax.random.fold_in(own_key, 6), axis_at), (parts,), jnp.float32, smallest / len(cuts), top_value / len(cuts))
        gain = gain * jnp.repeat(jnp.exp(steps), shape[axis_at] // parts).reshape((-1,) + (1,) * (len(shape) - 1 - axis_at))
    return gain


def bell_draw(rng, extent, width, most, cuts=(), kind=jnp.bfloat16):
    result = width * jax.random.normal(rng, extent, jnp.float32)
    if cuts:
        result = result * block_levels(rng, extent, cuts, -0.22, 0.18)
    return jnp.clip(result, -most, most).astype(kind)


def setup_inputs(seed: int = 0) -> dict:
    key_list = jax.random.split(jax.random.key(seed), 10)
    return {
        "tokens": bell_draw(key_list[0], (TOKENS, D), 1.0, 6.0, ((0, 256),)),
        "expert_ids": draw_expert_ids(jax.random.fold_in(key_list[9], 71), 0),
        "router_weight": bell_draw(key_list[2], (REPLICAS, EXPERTS, D), 1.0, 6.0, ((0, 4),)),
        "expert_weights": bell_draw(key_list[3], (REPLICAS, 3, D, FF), 1.0, 6.0, ((0, 4), (3, 64))),
        "outer_params": bell_draw(key_list[4], (FR, FF), 1.0, 6.0, ((1, 64),), jnp.float32),
        "outer_momentum": bell_draw(key_list[5], (FR, FF), 0.2, 3.0, ((1, 64),), jnp.float32),
        "inner_drift": bell_draw(key_list[6], (REPLICAS, FR, FF), 0.2, 3.0, ((0, 4), (2, 64)), jnp.float32),
        "frag_index": jax.random.randint(key_list[7], (1,), 0, NFRAG).astype(jnp.int32),
        "out_grad": bell_draw(key_list[8], (TOKENS, D), 1.0, 6.0, ((0, 256),)),
    }


inner_rate = 2.0
outer_rate = 0.7
momentum_decay = 0.9

def from_rows(left, right, factor, offset):
    part = lax.dynamic_slice_in_dim(left, offset, FR, 1)
    return lax.dot_general(part, right, (((0,), (0,)), ((), ())), preferred_element_type=jnp.float32) * factor

def group_pass(tokens, expert_ids, router, weights, frag, out_grad):
    scale_in = 1.0 / math.sqrt(D)
    scale_hid = 1.0 / math.sqrt(FF)
    routed = (expert_ids[:, 0] == 0) | (expert_ids[:, 1] == 0)
    index = jnp.nonzero(routed, size=N_FSDP * CAP)[0].astype(jnp.int32)
    other = (expert_ids[:, 0] + expert_ids[:, 1])[index].astype(jnp.int32)
    rows_in = tokens[index]
    grad_tok = out_grad[index].astype(jnp.float32)
    logits = jnp.dot(rows_in, router.T, preferred_element_type=jnp.float32) * scale_in
    logit_other = jnp.take_along_axis(logits, other[:, None], axis=1)[:, 0]
    prob = jax.nn.sigmoid(logits[:, 0] - logit_other)
    gate = jnp.dot(rows_in, weights[0], preferred_element_type=jnp.float32) * scale_in
    up = jnp.dot(rows_in, weights[1], preferred_element_type=jnp.float32) * scale_in
    sigma = jax.nn.sigmoid(gate)
    active = gate * sigma
    hidden = (active * up).astype(jnp.bfloat16)
    contract = (((1,), (1,)), ((), ()))
    outputs = lax.dot_general(hidden, weights[2], contract, preferred_element_type=jnp.float32) * scale_hid
    mixed_rows = (prob[:, None] * outputs).astype(jnp.bfloat16)
    rows_grad = (prob[:, None] * grad_tok).astype(jnp.bfloat16)
    d_hidden = jnp.dot(rows_grad, weights[2], preferred_element_type=jnp.float32) * scale_hid
    d_gate = (d_hidden * up * (sigma + gate * sigma * (1.0 - sigma))).astype(jnp.bfloat16)
    d_up = (d_hidden * active).astype(jnp.bfloat16)
    d_rows = (lax.dot_general(d_gate, weights[0], contract, preferred_element_type=jnp.float32) + lax.dot_general(d_up, weights[1], contract, preferred_element_type=jnp.float32)) * scale_in
    d_prob = lax.optimization_barrier(jnp.sum(grad_tok * outputs, axis=1))
    d_logit = d_prob * prob * (1.0 - prob)
    router_f = router.astype(jnp.float32)
    differ = router_f[0][None, :] - router_f[other]
    grad_rows = (d_rows + (d_logit * scale_in)[:, None] * differ).astype(jnp.bfloat16)
    count = tokens.shape[0]
    expert_out = jnp.zeros((count, D), jnp.bfloat16).at[index].set(mixed_rows)
    token_grad = jnp.zeros((count, D), jnp.bfloat16).at[index].set(grad_rows)
    per_mat = D // FR
    matrix = frag // per_mat
    offset = (frag % per_mat * FR).astype(jnp.int32)
    frag_grad = lax.switch(matrix, [partial(from_rows, rows_in, d_gate, scale_in, offset), partial(from_rows, rows_in, d_up, scale_in, offset), partial(from_rows, rows_grad, hidden, scale_hid, offset)])
    return (expert_out, token_grad, frag_grad)

def reference(tokens, expert_ids, router_weight, expert_weights, outer_params, outer_momentum, inner_drift, frag_index, out_grad):
    group = TOKENS // N_REPLICA
    frag = frag_index[0]
    mixed_all = []
    grads_all = []
    pseudo = jnp.zeros((FR, FF), jnp.float32)
    for member in range(N_REPLICA):
        lower = member * group
        upper = lower + group
        mixed, token_grad, frag_grad = group_pass(tokens[lower:upper], expert_ids[lower:upper], router_weight[member], expert_weights[member], frag, out_grad[lower:upper])
        mixed_all.append(mixed)
        grads_all.append(token_grad)
        pseudo = pseudo + (inner_rate * frag_grad - inner_drift[member])
    pseudo = pseudo / N_REPLICA
    new_momentum = momentum_decay * outer_momentum + pseudo
    new_params = outer_params - outer_rate * (pseudo + momentum_decay * new_momentum)
    return (jnp.concatenate(mixed_all, axis=0), jnp.concatenate(grads_all, axis=0), new_params, new_momentum)
```

```python
import math

import jax
import jax.numpy as jnp
from jax import lax
from jax.experimental import pallas as pl
from jax.experimental.pallas import tpu as pltpu
from jax.sharding import PartitionSpec as P

D = 6144
FF = 8192
EXPERTS = 8
CAP = 3
FR = 768
TOK = 64
KC = 16
LC = D // KC
BR = CAP * KC
NX = 4
NY = 4
NZ = 2
HID = 128
PLANE_TOK = 96
ROWS = 192
QR = FR // 4

inner_rate = 2.0
outer_rate = 0.7
momentum_decay = 0.9
scale_in = 1.0 / math.sqrt(D)
scale_hid = 1.0 / math.sqrt(FF)

MESH = pl.DeviceIdType.MESH
F32 = jnp.float32
BF16 = jnp.bfloat16
NT = (((1,), (1,)), ((), ()))
TN = (((0,), (0,)), ((), ()))


def dot(a, b, dims=(((1,), (0,)), ((), ()))):
    return lax.dot_general(a, b, dims, preferred_element_type=F32)


def iota(shape, dim):
    return lax.broadcasted_iota(jnp.int32, shape, dim)


def one(mask):
    return jnp.where(mask, 1.0, 0.0)


def row(slab, z, p):
    return ((slab * NZ + z) * 4 + p) * BR


def id_rows(ids):
    id0, id1 = ids[0:1, :], ids[1:2, :]
    at = iota((16, TOK), 0)
    routed = one((id0 == 0) | (id1 == 0))
    other = (id0 + id1).astype(F32)
    return jnp.where(at == 0, routed, jnp.where(at == 1, other, 0.0)).astype(BF16)


def kernel(
    tokens,
    ids,
    router,
    weights,
    drift,
    frag,
    grads,
    out_rows,
    out_pseudo,
    tokv,
    grdv,
    wgu,
    wdn,
    drfv,
    perm,
    ag,
    xv,
    gv,
    yv,
    rb,
    sb,
    t2,
    d2,
    t1,
    d1,
    zr,
    fq,
    fb,
    fr,
    ps,
    load_sem,
    ag_recv,
    z_send,
    r1_send,
    r2_send,
    sib_send,
    rs_sib_send,
    rs_sib_recv,
    t2_send,
    t2_recv,
    d2_send,
    d2_recv,
    t1_send,
    t1_recv,
    d1_send,
    d1_recv,
    zr_send,
    zr_recv,
    q_send,
    q_recv,
    p_send,
    p_recv,
):
    rep = lax.axis_index("replica")
    me = lax.axis_index("fsdp")
    core = me % 2
    py = (me // 2) % NY
    px = (me // (2 * NY)) % NX
    pz = me // (2 * NY * NX)
    first = 1 - core

    def dev(z, x, y, c):
        return {"fsdp": ((z * NX + x) * NY + y) * 2 + c}

    def ring_x(step):
        return dev(pz, (px + step) % NX, py, core)

    def ring_y(step):
        return dev(pz, px, (py + step) % NY, core)

    def pick(a, b):
        return {"fsdp": first * a["fsdp"] + core * b["fsdp"]}

    up1, dn1 = pick(ring_x(1), ring_y(1)), pick(ring_x(3), ring_y(3))
    up2, dn2 = pick(ring_y(1), ring_x(1)), pick(ring_y(3), ring_x(3))
    zpart = dev(1 - pz, px, py, core)
    sib = dev(pz, px, py, 1 - core)
    reps = [{"replica": (rep + d) % 4} for d in (1, 2, 3)]

    def load(src, dst, i):
        c = pltpu.make_async_copy(src, dst, load_sem.at[i])
        c.start()
        return c

    load_tok = load(tokens, tokv, 0)
    load_grd = load(grads, grdv, 1)

    barrier = pltpu.get_barrier_semaphore()
    peers = [up1, dn1, up2, dn2, zpart, sib] + reps
    for p in peers:
        pl.semaphore_signal(barrier, inc=1, device_id=p, device_id_type=MESH)

    load_g = load(weights.at[0, 0], wgu.at[:, 0:HID], 2)
    load_u = load(weights.at[0, 1], wgu.at[:, HID : 2 * HID], 3)
    load_d = load(weights.at[0, 2], wdn, 4)
    load_f = load(drift.at[0], drfv, 5)

    def send(src, dst, ssem, rsem, to):
        c = pltpu.make_async_remote_copy(
            src_ref=src, dst_ref=dst, send_sem=ssem, recv_sem=rsem,
            device_id=to, device_id_type=MESH,
        )
        c.start()
        return c

    def arrived(dst, rsem):
        pltpu.make_async_copy(dst, dst, rsem).wait()

    pending = []

    rows8 = id_rows(ids)
    wide = (TOK, KC * TOK)
    tiled = dot(rows8, one(iota(wide, 0) == iota(wide, 1) % TOK).astype(BF16))
    count = dot(rows8, one(iota(wide, 0) <= iota(wide, 1) % TOK).astype(BF16))
    sshape = (BR, KC * TOK)
    smask = (
        (tiled[0:1] > 0.5)
        & (count[0:1] - 1.0 == (iota(sshape, 0) // KC).astype(F32))
        & (iota(sshape, 0) % KC == iota(sshape, 1) // TOK)
    )
    select = one(smask).astype(BF16)
    other48 = jnp.sum(jnp.where(smask, tiled[1:2], 0.0), axis=1, keepdims=True)
    dshape = (BR, KC * EXPERTS)
    expert = iota(dshape, 1) % EXPERTS
    signs = jnp.where(
        iota(dshape, 0) % KC == iota(dshape, 1) // EXPERTS,
        one(expert == 0) - one(expert.astype(F32) == other48),
        0.0,
    ).astype(BF16)
    rw = router[0].astype(F32)
    router2 = jnp.concatenate([rw[:, k * LC : (k + 1) * LC] for k in range(KC)], axis=0)
    differ = dot(signs, router2.astype(BF16))

    pshape = (256, 256)
    perm[...] = one(
        (iota(pshape, 0) // 16 == iota(pshape, 1) % 16)
        & (iota(pshape, 0) % 16 == iota(pshape, 1) // 16)
    ).astype(BF16)

    def fold(ref):
        stacked = jnp.concatenate([ref[:, k * LC : (k + 1) * LC] for k in range(KC)], axis=0)
        return dot(select, stacked)

    load_tok.wait()
    xsel = fold(tokv)
    ag[0, 0, 0:BR, :] = xsel.astype(BF16)
    logit = jnp.sum((xsel * differ).reshape(CAP, KC, LC), axis=(1, 2), keepdims=True)
    prob = jax.nn.sigmoid(jnp.broadcast_to(logit * scale_in, (CAP, KC, LC)).reshape(BR, LC))
    load_grd.wait()
    gsel = fold(grdv)
    ag[1, 0, 0:BR, :] = (prob * gsel).astype(BF16)

    pl.semaphore_wait(barrier, len(peers))

    def piece(plane, slab, z, p):
        return ag.at[:, plane, pl.ds(row(slab, z, p), BR), :]

    def ag_sem(plane, slab, z, p):
        return ag_recv.at[((plane * 4 + slab) * 2 + z) * 4 + p]

    def push(src_key, dst_key, ssem, to):
        pending.append(send(piece(*src_key), piece(*dst_key), ssem, ag_sem(*dst_key), to))

    def to_sib(slab, z, p):
        push((0, slab, z, p), (1, slab, z, p), sib_send.at[(slab * 2 + z) * 4 + p], sib)

    def to_ring2(z, p):
        i = z * 4 + p
        push((0, 0, z, p), (0, 3, z, p), r2_send.at[i], up2)
        push((0, 0, z, p), (0, 1, z, p), r2_send.at[8 + i], dn2)

    def to_ring1(z):
        push((0, 0, z, 0), (0, 0, z, 3), r1_send.at[z], up1)
        push((0, 0, z, 0), (0, 0, z, 1), r1_send.at[2 + z], dn1)

    def got(plane, slab, z, p):
        arrived(piece(plane, slab, z, p), ag_sem(plane, slab, z, p))

    push((0, 0, 0, 0), (0, 0, 1, 0), z_send, zpart)
    to_ring1(0)
    to_ring2(0, 0)
    to_sib(0, 0, 0)
    got(0, 0, 1, 0)
    to_ring1(1)
    to_ring2(1, 0)
    to_sib(0, 1, 0)
    order = [(0, 0), (1, 0), (0, 3), (0, 1), (1, 1), (1, 3), (0, 2), (1, 2)]
    for z, p in order[2:]:
        got(0, 0, z, p)
        if (z, p) == (0, 3):
            push((0, 0, 0, 3), (0, 0, 0, 2), r1_send.at[4], up1)
        if (z, p) == (1, 1):
            push((0, 0, 1, 1), (0, 0, 1, 2), r1_send.at[5], dn1)
        to_ring2(z, p)
        to_sib(0, z, p)
    for z, p in order:
        got(0, 3, z, p)
        if z == 0:
            push((0, 3, 0, p), (0, 2, 0, p), r2_send.at[16 + p], up2)
        to_sib(3, z, p)
        got(0, 1, z, p)
        if z == 1:
            push((0, 1, 1, p), (0, 2, 1, p), r2_send.at[20 + p], dn2)
        to_sib(1, z, p)

    def unfold(plane, lo, hi):
        @pl.loop(lo, hi)
        def _(g):
            rows_at = pl.ds(pl.multiple_of(plane * PLANE_TOK + g * 16, 16), 16)
            for i, dst in ((0, xv), (1, gv)):
                v = ag[i, plane, pl.ds(pl.multiple_of(g * 256, 256), 256), :]
                r = dot(perm[...], v).astype(BF16)
                for k in range(KC):
                    dst[rows_at, k * LC : (k + 1) * LC] = r[16 * k : 16 * k + 16]

    unfold(0, 0, 3)
    for z, p in order:
        got(0, 2, z, p)
        to_sib(2, z, p)
    unfold(0, 3, 6)
    for slab in (0, 3, 1, 2):
        for z, p in order:
            got(1, slab, z, p)
        if slab == 1:
            unfold(1, 0, 3)
    unfold(1, 3, 6)

    load_g.wait()
    load_u.wait()
    load_d.wait()
    gu = dot(xv[...], wgu[...]) * scale_in
    gate, up = gu[:, :HID], gu[:, HID:]
    d_hidden = dot(gv[...], wdn[...]) * scale_hid
    sigma = jax.nn.sigmoid(gate)
    active = gate * sigma
    hidden = (active * up).astype(BF16)
    d_gate = (d_hidden * up * (sigma + gate * sigma * (1.0 - sigma))).astype(BF16)
    d_up = (d_hidden * active).astype(BF16)
    d_gu = jnp.concatenate([d_gate, d_up], axis=1)

    def back(plane):
        lo = plane * PLANE_TOK
        h = hidden[lo : lo + PLANE_TOK]
        dg = d_gu[lo : lo + PLANE_TOK]
        for k in range(KC):
            w = pl.ds(k * LC, LC)
            yv[0, k] = (dot(h, wdn[w, :], NT) * scale_hid).astype(BF16)
            yv[1, k] = (dot(dg, wgu[w, :], NT) * scale_in).astype(BF16)

    def refold(plane, lo, hi):
        @pl.loop(lo, hi)
        def _(g):
            at = pl.ds(pl.multiple_of(g * 16, 16), 16)
            for i in range(2):
                v = yv[i, :, at, :].reshape(256, LC)
                rb[i, plane, pl.ds(pl.multiple_of(g * 256, 256), 256), :] = dot(
                    perm[...], v
                ).astype(BF16)

    def region(ref, lo, n):
        return ref.at[:, pl.ds(lo, n), :]

    HALF = 4 * BR

    def rs_to_sib(slab, z):
        i = slab * 2 + z
        src = rb.at[:, 1, pl.ds(row(slab, z, 0), HALF), :]
        dst = region(sb, row(slab, z, 0), HALF)
        pending.append(send(src, dst, rs_sib_send.at[i], rs_sib_recv.at[i], sib))

    back(1)
    refold(1, 3, 6)
    for slab in (2, 3):
        for z in range(2):
            rs_to_sib(slab, z)
    refold(1, 0, 3)
    for slab in (1, 0):
        for z in range(2):
            rs_to_sib(slab, z)
    back(0)
    refold(0, 3, 6)
    refold(0, 0, 3)

    def add_sib(slab, z):
        lo = row(slab, z, 0)
        arrived(region(sb, lo, HALF), rs_sib_recv.at[slab * 2 + z])
        for i in range(2):
            for p in range(4):
                at = pl.ds(lo + p * BR, BR)
                rb[i, 0, at, :] = (rb[i, 0, at, :].astype(F32) + sb[i, at, :].astype(F32)).astype(
                    BF16
                )

    def mine(slab, z, p):
        return rb.at[:, 0, pl.ds(row(slab, z, p), BR), :]

    def send_t2(way, p, to):
        src = mine(2, way, p)
        i = way * 4 + p
        pending.append(
            send(src, region(t2.at[way], p * BR, BR), t2_send.at[i], t2_recv.at[i], to)
        )

    def send_d2(way, slab, z, p, to):
        i = (way * 2 + z) * 4 + p
        dst = region(d2.at[way], (z * 4 + p) * BR, BR)
        pending.append(send(mine(slab, z, p), dst, d2_send.at[i], d2_recv.at[i], to))

    porder = (2, 1, 3, 0)
    add_sib(2, 0)
    for p in porder:
        send_t2(0, p, up2)
    add_sib(2, 1)
    for p in porder:
        send_t2(1, p, dn2)
    add_sib(3, 0)
    for p in porder:
        send_d2(1, 3, 0, p, dn2)
    add_sib(1, 1)
    for p in porder:
        send_d2(0, 1, 1, p, up2)

    which = frag[...]
    per = D // FR
    masks = [one((which >= m * per) & (which < (m + 1) * per)) for m in range(3)]
    left = jnp.zeros((ROWS, FR), BF16)
    for src, off in ((xv, 1.0 - masks[2]), (gv, masks[2])):
        for c in range(per):
            here = one((which == c) | (which == per + c) | (which == 2 * per + c))
            left = left + src[:, c * FR : (c + 1) * FR] * (off * here).astype(BF16)
    right = (
        d_gate * masks[0].astype(BF16)
        + d_up * masks[1].astype(BF16)
        + hidden * masks[2].astype(BF16)
    )
    factor = inner_rate * (scale_in * (1.0 - masks[2]) + scale_hid * masks[2])
    load_f.wait()
    fq[...] = dot(left, right, TN) * factor - drfv[...]
    fb[...] = fq[...].astype(BF16)
    for d in range(3):
        at = pl.ds(pl.multiple_of(((rep + d + 1) % 4) * QR, 64), QR)
        pending.append(send(fb.at[at, :], fr.at[d], q_send.at[d], q_recv.at[d], reps[d]))

    add_sib(1, 0)
    add_sib(3, 1)

    def add_into(slab, z, p, *others):
        at = pl.ds(row(slab, z, p), BR)
        for i in range(2):
            v = rb[i, 0, at, :].astype(F32)
            for ref, lo in others:
                v = v + ref[i, pl.ds(lo, BR), :].astype(F32)
            rb[i, 0, at, :] = v.astype(BF16)

    for p in porder:
        arrived(region(t2.at[0], p * BR, BR), t2_recv.at[p])
        add_into(1, 0, p, (t2.at[0], p * BR))
        send_d2(0, 1, 0, p, up2)
        arrived(region(t2.at[1], p * BR, BR), t2_recv.at[4 + p])
        add_into(3, 1, p, (t2.at[1], p * BR))
        send_d2(1, 3, 1, p, dn2)
    add_sib(0, 0)
    add_sib(0, 1)

    for d in range(3):
        arrived(fr.at[d], q_recv.at[d])
    own = pl.ds(pl.multiple_of(rep * QR, 64), QR)
    total = fq[own, :]
    for d in range(3):
        total = total + fr[d].astype(F32)
    ps[own, :] = (total * 0.25).astype(BF16)
    for d in range(3):
        pending.append(send(ps.at[own, :], ps.at[own, :], p_send.at[d], p_recv.at[d], reps[d]))

    def finish2(z, p):
        lo = (z * 4 + p) * BR
        for way in range(2):
            arrived(region(d2.at[way], lo, BR), d2_recv.at[(way * 2 + z) * 4 + p])
        add_into(0, z, p, (d2.at[0], lo), (d2.at[1], lo))

    def send_t1(way, to):
        pending.append(
            send(mine(0, way, 2), t1.at[way], t1_send.at[way], t1_recv.at[way], to)
        )

    def send_d1(way, z, p, to):
        i = way * 2 + z
        dst = region(d1.at[way], z * BR, BR)
        pending.append(send(mine(0, z, p), dst, d1_send.at[i], d1_recv.at[i], to))

    finish2(0, 2)
    send_t1(0, up1)
    finish2(1, 2)
    send_t1(1, dn1)
    finish2(1, 1)
    send_d1(0, 1, 1, up1)
    finish2(0, 3)
    send_d1(1, 0, 3, dn1)
    finish2(0, 1)
    arrived(t1.at[0], t1_recv.at[0])
    add_into(0, 0, 1, (t1.at[0], 0))
    send_d1(0, 0, 1, up1)
    finish2(1, 3)
    arrived(t1.at[1], t1_recv.at[1])
    add_into(0, 1, 3, (t1.at[1], 0))
    send_d1(1, 1, 3, dn1)
    finish2(1, 0)
    finish2(0, 0)

    def finish1(z):
        for way in range(2):
            arrived(region(d1.at[way], z * BR, BR), d1_recv.at[way * 2 + z])
        add_into(0, z, 0, (d1.at[0], z * BR), (d1.at[1], z * BR))

    finish1(1)
    pending.append(send(mine(0, 1, 0), zr, zr_send, zr_recv, zpart))

    for d in range(3):
        at = pl.ds(pl.multiple_of(((rep + 3 - d) % 4) * QR, 64), QR)
        arrived(ps.at[at, :], p_recv.at[d])
    out_pseudo[...] = ps[...]

    finish1(0)
    arrived(zr, zr_recv)
    y = rb[0, 0, 0:BR, :].astype(F32) + zr[0].astype(F32)
    dx = rb[1, 0, 0:BR, :].astype(F32) + zr[1].astype(F32)
    d_prob = jnp.sum((gsel * y).reshape(CAP, KC, LC), axis=(1, 2), keepdims=True)
    d_prob = jnp.broadcast_to(d_prob, (CAP, KC, LC)).reshape(BR, LC)
    d_logit = d_prob * prob * (1.0 - prob)
    out_rows[0] = (prob * y).astype(BF16)
    out_rows[1] = (dx + (d_logit * scale_in) * differ).astype(BF16)

    for c in pending:
        c.wait_send()


def finish(
    ids, rows_hbm, pseudo_hbm, params, momentum,
    out_mixed, out_grad, out_params, out_momentum,
    rows, pseudo, mixv, grdv, parv, momv, sem,
):
    def store(src, dst, i):
        c = pltpu.make_async_copy(src, dst, sem.at[i])
        c.start()
        return c

    load_pseudo = store(pseudo_hbm, pseudo, 4)
    load_rows = store(rows_hbm, rows, 5)
    load_pseudo.wait()
    shift = pseudo[...].astype(F32)
    mom = momentum_decay * momentum[...] + shift
    momv[...] = mom
    stores = [store(momv, out_momentum, 0)]
    parv[...] = params[...] - outer_rate * (shift + momentum_decay * mom)
    stores.append(store(parv, out_params, 1))

    rows8 = id_rows(ids)
    tri = one(iota((TOK, TOK), 0) >= iota((TOK, TOK), 1)).astype(BF16)
    eye = one(iota((TOK, TOK), 0) == iota((TOK, TOK), 1)).astype(BF16)
    slot = dot(tri, rows8, NT)[:, 0:1] - 1.0
    routed = dot(eye, rows8, NT)[:, 0:1]
    shape = (TOK, BR)
    mine = (slot == (iota(shape, 1) // KC).astype(F32)) & (routed > 0.5)
    spread = jnp.concatenate(
        [one(mine & (iota(shape, 1) % KC == k)).astype(BF16) for k in range(KC)], axis=0
    )
    load_rows.wait()
    for src, buf, dst in ((0, mixv, out_mixed), (1, grdv, out_grad)):
        placed = dot(spread, rows[src]).astype(BF16)
        for k in range(KC):
            buf[:, k * LC : (k + 1) * LC] = placed[k * TOK : (k + 1) * TOK]
        stores.append(store(buf, dst, 2 + src))
    for c in stores:
        c.wait()


def body(
    tokens,
    expert_ids,
    router_weight,
    expert_weights,
    outer_params,
    outer_momentum,
    inner_drift,
    frag_index,
    out_grad,
):
    vmem = pl.BlockSpec(memory_space=pltpu.VMEM)
    anyw = pl.BlockSpec(memory_space=pl.ANY)
    dma = pltpu.SemaphoreType.DMA
    scratch = [
        pltpu.VMEM((TOK, D), BF16),
        pltpu.VMEM((TOK, D), BF16),
        pltpu.VMEM((D, 2 * HID), BF16),
        pltpu.VMEM((D, HID), BF16),
        pltpu.VMEM((FR, HID), F32),
        pltpu.VMEM((256, 256), BF16),
        pltpu.VMEM((2, 2, PLANE_TOK * KC, LC), BF16),
        pltpu.VMEM((ROWS, D), BF16),
        pltpu.VMEM((ROWS, D), BF16),
        pltpu.VMEM((2, KC, PLANE_TOK, LC), BF16),
        pltpu.VMEM((2, 2, PLANE_TOK * KC, LC), BF16),
        pltpu.VMEM((2, PLANE_TOK * KC, LC), BF16),
        pltpu.VMEM((2, 2, 4 * BR, LC), BF16),
        pltpu.VMEM((2, 2, 8 * BR, LC), BF16),
        pltpu.VMEM((2, 2, BR, LC), BF16),
        pltpu.VMEM((2, 2, 2 * BR, LC), BF16),
        pltpu.VMEM((2, BR, LC), BF16),
        pltpu.VMEM((FR, HID), F32),
        pltpu.VMEM((FR, HID), BF16),
        pltpu.VMEM((3, QR, HID), BF16),
        pltpu.VMEM((FR, HID), BF16),
        dma((6,)),
        dma((64,)),
        dma,
        dma((6,)),
        dma((24,)),
        dma((32,)),
        dma((8,)),
        dma((8,)),
        dma((8,)),
        dma((8,)),
        dma((16,)),
        dma((16,)),
        dma((2,)),
        dma((2,)),
        dma((4,)),
        dma((4,)),
        dma,
        dma,
        dma((3,)),
        dma((3,)),
        dma((3,)),
        dma((3,)),
    ]
    ids = expert_ids.T
    rows, pseudo = pl.pallas_call(
        kernel,
        out_shape=(
            jax.ShapeDtypeStruct((2, BR, LC), BF16),
            jax.ShapeDtypeStruct((FR, HID), BF16),
        ),
        in_specs=[anyw, vmem, vmem, anyw, anyw, vmem, anyw],
        out_specs=(vmem, vmem),
        scratch_shapes=scratch,
        compiler_params=pltpu.CompilerParams(
            collective_id=0, has_side_effects=True, vmem_limit_bytes=56 * 1024 * 1024
        ),
        cost_estimate=pl.CostEstimate(
            flops=4_000_000_000, bytes_accessed=12_000_000, transcendentals=100_000
        ),
    )(
        tokens,
        ids,
        router_weight,
        expert_weights,
        inner_drift,
        frag_index.reshape(1, 1),
        out_grad,
    )
    return pl.pallas_call(
        finish,
        out_shape=(
            jax.ShapeDtypeStruct((TOK, D), BF16),
            jax.ShapeDtypeStruct((TOK, D), BF16),
            jax.ShapeDtypeStruct((FR, HID), F32),
            jax.ShapeDtypeStruct((FR, HID), F32),
        ),
        in_specs=[vmem, anyw, anyw, vmem, vmem],
        out_specs=(anyw, anyw, anyw, anyw),
        scratch_shapes=[
            pltpu.VMEM((2, BR, LC), BF16),
            pltpu.VMEM((FR, HID), BF16),
            pltpu.VMEM((TOK, D), BF16),
            pltpu.VMEM((TOK, D), BF16),
            pltpu.VMEM((FR, HID), F32),
            pltpu.VMEM((FR, HID), F32),
            dma((6,)),
        ],
        compiler_params=pltpu.CompilerParams(vmem_limit_bytes=16 * 1024 * 1024),
    )(ids, rows, pseudo, outer_params, outer_momentum)


def solution(mesh):
    in_specs = (
        P(("replica", "fsdp"), None),
        P(("replica", "fsdp"), None),
        P("replica", None, None),
        P("replica", None, None, "fsdp"),
        P(None, "fsdp"),
        P(None, "fsdp"),
        P("replica", None, "fsdp"),
        P(),
        P(("replica", "fsdp"), None),
    )
    out_specs = (
        P(("replica", "fsdp"), None),
        P(("replica", "fsdp"), None),
        P(None, "fsdp"),
        P(None, "fsdp"),
    )
    return jax.shard_map(body, mesh=mesh, in_specs=in_specs, out_specs=out_specs, check_vma=False)
```

```python
import math

import jax
import jax.numpy as jnp
from jax import lax
from jax.experimental import pallas as pl
from jax.experimental.pallas import tpu as pltpu
from jax.sharding import PartitionSpec as P

D = 6144
FF = 8192
EXPERTS = 8
CAP = 3
FR = 768
TOK = 64
KC = 16
LC = D // KC
BR = CAP * KC
NX = 4
NY = 4
NZ = 2
HID = 128
ROWS = 96
QR = FR // 4

inner_rate = 2.0
outer_rate = 0.7
momentum_decay = 0.9
scale_in = 1.0 / math.sqrt(D)
scale_hid = 1.0 / math.sqrt(FF)

MESH = pl.DeviceIdType.MESH
F32 = jnp.float32
BF16 = jnp.bfloat16
NT = (((1,), (1,)), ((), ()))
TN = (((0,), (0,)), ((), ()))


def dot(a, b, dims=(((1,), (0,)), ((), ()))):
    return lax.dot_general(a, b, dims, preferred_element_type=F32)


def iota(shape, dim):
    return lax.broadcasted_iota(jnp.int32, shape, dim)


def one(mask):
    return jnp.where(mask, 1.0, 0.0)


def row(slab, z, p):
    return ((slab * NZ + z) * 4 + p) * BR


def id_rows(ids):
    id0, id1 = ids[0:1, :], ids[1:2, :]
    at = iota((16, TOK), 0)
    routed = one((id0 == 0) | (id1 == 0))
    other = (id0 + id1).astype(F32)
    return jnp.where(at == 0, routed, jnp.where(at == 1, other, 0.0)).astype(BF16)


def kernel(
    tokens,
    ids,
    router,
    weights,
    drift,
    frag,
    grads,
    out_rows,
    out_pseudo,
    tokv,
    grdv,
    wgu,
    wdn,
    drfv,
    perm,
    ag,
    xv,
    gv,
    yv,
    rb,
    t2,
    d2,
    e1,
    fq,
    fb,
    fs,
    fh,
    fr,
    ps,
    load_sem,
    ag_recv,
    r1_send,
    r2_send,
    w_send,
    w_recv,
    t2_send,
    t2_recv,
    d2_send,
    d2_recv,
    e1_send,
    e1_recv,
    f_send,
    f_recv,
    q_send,
    q_recv,
    p_send,
    p_recv,
):
    rep = lax.axis_index("replica")
    me = lax.axis_index("fsdp")
    core = me % 2
    py = (me // 2) % NY
    px = (me // (2 * NY)) % NX
    pz = me // (2 * NY * NX)
    first = 1 - core

    def dev(z, x, y, c):
        return {"fsdp": ((z * NX + x) * NY + y) * 2 + c}

    def at1(z, step):
        x = (px + first * step) % NX
        y = (py + core * step) % NY
        return dev((pz + z) % NZ, x, y, core)

    def at2(step):
        return dev(pz, (px + core * step) % NX, (py + first * step) % NY, core)

    up2, dn2 = at2(1), at2(3)
    sib = dev(pz, px, py, 1 - core)
    near = {(z, p): at1(z, p) for z in range(NZ) for p in range(4) if (z, p) != (0, 0)}
    reps = [{"replica": (rep + d) % 4} for d in (1, 2, 3)]

    def load(src, dst, i):
        c = pltpu.make_async_copy(src, dst, load_sem.at[i])
        c.start()
        return c

    load_tok = load(tokens, tokv, 0)
    load_grd = load(grads, grdv, 1)

    barrier = pltpu.get_barrier_semaphore()
    peers = [up2, dn2, sib] + list(near.values()) + reps
    for p in peers:
        pl.semaphore_signal(barrier, inc=1, device_id=p, device_id_type=MESH)

    def send(src, dst, ssem, rsem, to):
        c = pltpu.make_async_remote_copy(
            src_ref=src, dst_ref=dst, send_sem=ssem, recv_sem=rsem,
            device_id=to, device_id_type=MESH,
        )
        c.start()
        return c

    def arrived(dst, rsem):
        pltpu.make_async_copy(dst, dst, rsem).wait()

    pending = []

    rows8 = id_rows(ids)
    wide = (TOK, KC * TOK)
    tiled = dot(rows8, one(iota(wide, 0) == iota(wide, 1) % TOK).astype(BF16))
    count = dot(rows8, one(iota(wide, 0) <= iota(wide, 1) % TOK).astype(BF16))
    sshape = (BR, KC * TOK)
    smask = (
        (tiled[0:1] > 0.5)
        & (count[0:1] - 1.0 == (iota(sshape, 0) // KC).astype(F32))
        & (iota(sshape, 0) % KC == iota(sshape, 1) // TOK)
    )
    select = one(smask).astype(BF16)
    other48 = jnp.sum(jnp.where(smask, tiled[1:2], 0.0), axis=1, keepdims=True)
    dshape = (BR, KC * EXPERTS)
    expert = iota(dshape, 1) % EXPERTS
    signs = jnp.where(
        iota(dshape, 0) % KC == iota(dshape, 1) // EXPERTS,
        one(expert == 0) - one(expert.astype(F32) == other48),
        0.0,
    ).astype(BF16)
    rw = router[0].astype(F32)
    router2 = jnp.concatenate([rw[:, k * LC : (k + 1) * LC] for k in range(KC)], axis=0)
    differ = dot(signs, router2.astype(BF16))

    pshape = (256, 256)
    perm[...] = one(
        (iota(pshape, 0) // 16 == iota(pshape, 1) % 16)
        & (iota(pshape, 0) % 16 == iota(pshape, 1) // 16)
    ).astype(BF16)

    def fold(ref):
        stacked = jnp.concatenate([ref[:, k * LC : (k + 1) * LC] for k in range(KC)], axis=0)
        return dot(select, stacked)

    load_tok.wait()
    xsel = fold(tokv)
    ag[0, 0:BR, :] = xsel.astype(BF16)
    logit = jnp.sum((xsel * differ).reshape(CAP, KC, LC), axis=(1, 2), keepdims=True)
    prob = jax.nn.sigmoid(jnp.broadcast_to(logit * scale_in, (CAP, KC, LC)).reshape(BR, LC))
    load_grd.wait()
    gsel = fold(grdv)
    ag[1, 0:BR, :] = (prob * gsel).astype(BF16)

    pl.semaphore_wait(barrier, len(peers))

    def piece(ref, slab, z, p):
        return ref.at[:, pl.ds(row(slab, z, p), BR), :]

    def ag_sem(slab, z, p):
        return ag_recv.at[(slab * 2 + z) * 4 + p]

    def push(src_key, dst_key, ssem, to):
        pending.append(send(piece(ag, *src_key), piece(ag, *dst_key), ssem, ag_sem(*dst_key), to))

    def to_ring2(z, p):
        i = z * 4 + p
        push((0, z, p), (3, z, p), r2_send.at[i], up2)
        push((0, z, p), (1, z, p), r2_send.at[8 + i], dn2)

    def got(slab, z, p):
        arrived(piece(ag, slab, z, p), ag_sem(slab, z, p))

    order = [(1, 0), (0, 3), (0, 1), (1, 1), (1, 3), (0, 2), (1, 2)]
    for z, p in order:
        push((0, 0, 0), (0, z, (4 - p) % 4), r1_send.at[z * 4 + p], near[z, p])
    to_ring2(0, 0)

    loads = []
    for m, (dst, lo, far) in enumerate(((wgu, 0, 2 * HID), (wgu, HID, 3 * HID), (wdn, 0, HID))):
        src = weights.at[0, m]
        loads.append(load(src, dst.at[:, lo : lo + HID], 2 + m))
        pending.append(send(src, dst.at[:, far : far + HID], w_send.at[m], w_recv.at[m], sib))
    load_f = load(drift.at[0], drfv, 5)

    for z, p in order:
        got(0, z, p)
        to_ring2(z, p)

    def unfold(lo, hi):
        @pl.loop(lo, hi)
        def _(g):
            rows_at = pl.ds(pl.multiple_of(g * 16, 16), 16)
            for i, dst in ((0, xv), (1, gv)):
                v = ag[i, pl.ds(pl.multiple_of(g * 256, 256), 256), :]
                r = dot(perm[...], v).astype(BF16)
                for k in range(KC):
                    dst[rows_at, k * LC : (k + 1) * LC] = r[16 * k : 16 * k + 16]

    for z, p in [(0, 0)] + order:
        got(3, z, p)
        if z == 0:
            push((3, 0, p), (2, 0, p), r2_send.at[16 + p], up2)
        got(1, z, p)
        if z == 1:
            push((1, 1, p), (2, 1, p), r2_send.at[20 + p], dn2)
    unfold(0, 3)
    for z, p in [(0, 0)] + order:
        got(2, z, p)
    unfold(3, 6)

    for c in loads:
        c.wait()
    for m, (dst, far) in enumerate(((wgu, 2 * HID), (wgu, 3 * HID), (wdn, HID))):
        arrived(dst.at[:, far : far + HID], w_recv.at[m])
    gu = dot(xv[...], wgu[...]) * scale_in
    gate = jnp.concatenate([gu[:, 0:HID], gu[:, 2 * HID : 3 * HID]], axis=1)
    up = jnp.concatenate([gu[:, HID : 2 * HID], gu[:, 3 * HID :]], axis=1)
    d_hidden = dot(gv[...], wdn[...]) * scale_hid
    sigma = jax.nn.sigmoid(gate)
    active = gate * sigma
    hidden = (active * up).astype(BF16)
    d_gate = (d_hidden * up * (sigma + gate * sigma * (1.0 - sigma))).astype(BF16)
    d_up = (d_hidden * active).astype(BF16)
    d_gu = jnp.concatenate(
        [d_gate[:, :HID], d_up[:, :HID], d_gate[:, HID:], d_up[:, HID:]], axis=1
    )

    for k in range(KC):
        w = pl.ds(k * LC, LC)
        yv[0, k] = (dot(hidden, wdn[w, :], NT) * scale_hid).astype(BF16)
        yv[1, k] = (dot(d_gu, wgu[w, :], NT) * scale_in).astype(BF16)

    def refold(lo, hi):
        @pl.loop(lo, hi)
        def _(g):
            at = pl.ds(pl.multiple_of(g * 16, 16), 16)
            for i in range(2):
                v = yv[i, :, at, :].reshape(256, LC)
                rb[i, pl.ds(pl.multiple_of(g * 256, 256), 256), :] = dot(perm[...], v).astype(BF16)

    def region(ref, lo, n):
        return ref.at[:, pl.ds(lo, n), :]

    def send_t2(way, p, to):
        i = way * 4 + p
        dst = region(t2.at[way], p * BR, BR)
        pending.append(send(piece(rb, 2, way, p), dst, t2_send.at[i], t2_recv.at[i], to))

    def send_d2(way, slab, z, p, to):
        i = (way * 2 + z) * 4 + p
        dst = region(d2.at[way], (z * 4 + p) * BR, BR)
        pending.append(send(piece(rb, slab, z, p), dst, d2_send.at[i], d2_recv.at[i], to))

    porder = (2, 1, 3, 0)
    refold(3, 6)
    for p in porder:
        send_t2(0, p, up2)
        send_t2(1, p, dn2)
    for p in porder:
        send_d2(1, 3, 0, p, dn2)
    refold(0, 3)
    for p in porder:
        send_d2(0, 1, 1, p, up2)

    which = frag[...]
    per = D // FR
    masks = [one((which >= m * per) & (which < (m + 1) * per)) for m in range(3)]
    left = jnp.zeros((ROWS, FR), BF16)
    for src, off in ((xv, 1.0 - masks[2]), (gv, masks[2])):
        for c in range(per):
            here = one((which == c) | (which == per + c) | (which == 2 * per + c))
            left = left + src[:, c * FR : (c + 1) * FR] * (off * here).astype(BF16)
    right = (
        d_gate * masks[0].astype(BF16)
        + d_up * masks[1].astype(BF16)
        + hidden * masks[2].astype(BF16)
    )
    factor = inner_rate * (scale_in * (1.0 - masks[2]) + scale_hid * masks[2])
    partial = dot(left, right, TN) * factor
    fb[...] = partial[:, HID:].astype(BF16)
    pending.append(send(fb, fs, f_send, f_recv, sib))
    load_f.wait()
    fq[...] = partial[:, :HID] - drfv[...]

    def add_into(slab, z, p, *others):
        at = pl.ds(row(slab, z, p), BR)
        for i in range(2):
            v = rb[i, at, :].astype(F32)
            for ref, lo in others:
                v = v + ref[i, pl.ds(lo, BR), :].astype(F32)
            rb[i, at, :] = v.astype(BF16)

    for j, p in enumerate(porder):
        arrived(region(t2.at[0], p * BR, BR), t2_recv.at[p])
        add_into(1, 0, p, (t2.at[0], p * BR))
        send_d2(0, 1, 0, p, up2)
        arrived(region(t2.at[1], p * BR, BR), t2_recv.at[4 + p])
        add_into(3, 1, p, (t2.at[1], p * BR))
        send_d2(1, 3, 1, p, dn2)
        if j == 1:
            arrived(fs, f_recv)
            fq[...] = fq[...] + fs[...].astype(F32)
            fh[...] = fq[...].astype(BF16)
            for d in range(3):
                at = pl.ds(pl.multiple_of(((rep + d + 1) % 4) * QR, 64), QR)
                pending.append(
                    send(fh.at[at, :], fr.at[d], q_send.at[d], q_recv.at[d], reps[d])
                )

    def finish2(z, p):
        lo = (z * 4 + p) * BR
        for way in range(2):
            arrived(region(d2.at[way], lo, BR), d2_recv.at[(way * 2 + z) * 4 + p])
        add_into(0, z, p, (d2.at[0], lo), (d2.at[1], lo))
        if (z, p) != (0, 0):
            i = z * 4 + (4 - p) % 4
            pending.append(
                send(piece(rb, 0, z, p), e1.at[i], e1_send.at[i], e1_recv.at[i], near[z, p])
            )

    for j, p in enumerate(porder):
        finish2(1, p)
        finish2(0, p)
        if j == 0:
            for d in range(3):
                arrived(fr.at[d], q_recv.at[d])
            own = pl.ds(pl.multiple_of(rep * QR, 64), QR)
            total = fq[own, :]
            for d in range(3):
                total = total + fr[d].astype(F32)
            ps[own, :] = (total * 0.25).astype(BF16)
            for d in range(3):
                pending.append(
                    send(ps.at[own, :], ps.at[own, :], p_send.at[d], p_recv.at[d], reps[d])
                )

    y = rb[0, 0:BR, :].astype(F32)
    dx = rb[1, 0:BR, :].astype(F32)
    for z, p in [(1, 0), (0, 1), (0, 3), (1, 1), (1, 3), (0, 2), (1, 2)]:
        i = z * 4 + p
        arrived(e1.at[i], e1_recv.at[i])
        y = y + e1[i, 0].astype(F32)
        dx = dx + e1[i, 1].astype(F32)
    d_prob = jnp.sum((gsel * y).reshape(CAP, KC, LC), axis=(1, 2), keepdims=True)
    d_prob = jnp.broadcast_to(d_prob, (CAP, KC, LC)).reshape(BR, LC)
    d_logit = d_prob * prob * (1.0 - prob)
    out_rows[0] = (prob * y).astype(BF16)
    out_rows[1] = (dx + (d_logit * scale_in) * differ).astype(BF16)

    for d in range(3):
        at = pl.ds(pl.multiple_of(((rep + 3 - d) % 4) * QR, 64), QR)
        arrived(ps.at[at, :], p_recv.at[d])
    out_pseudo[...] = ps[...]

    for c in pending:
        c.wait_send()


def finish(
    ids, rows_hbm, pseudo_hbm, params, momentum,
    out_mixed, out_grad, out_params, out_momentum,
    rows, pseudo, mixv, grdv, parv, momv, sem,
):
    def store(src, dst, i):
        c = pltpu.make_async_copy(src, dst, sem.at[i])
        c.start()
        return c

    load_rows = store(rows_hbm, rows, 5)
    loads = [store(pseudo_hbm, pseudo, 4), store(momentum, momv, 6), store(params, parv, 7)]

    rows8 = id_rows(ids)
    tri = one(iota((TOK, TOK), 0) >= iota((TOK, TOK), 1)).astype(BF16)
    eye = one(iota((TOK, TOK), 0) == iota((TOK, TOK), 1)).astype(BF16)
    slot = dot(tri, rows8, NT)[:, 0:1] - 1.0
    routed = dot(eye, rows8, NT)[:, 0:1]
    shape = (TOK, BR)
    mine = (slot == (iota(shape, 1) // KC).astype(F32)) & (routed > 0.5)
    spread = jnp.concatenate(
        [one(mine & (iota(shape, 1) % KC == k)).astype(BF16) for k in range(KC)], axis=0
    )
    stores = []
    load_rows.wait()
    for src, buf, dst in ((0, mixv, out_mixed), (1, grdv, out_grad)):
        placed = dot(spread, rows[src]).astype(BF16)
        for k in range(KC):
            buf[:, k * LC : (k + 1) * LC] = placed[k * TOK : (k + 1) * TOK]
        stores.append(store(buf, dst, 2 + src))
    for c in loads:
        c.wait()
    shift = pseudo[...].astype(F32)
    mom = momentum_decay * momv[...] + shift
    momv[...] = mom
    stores.append(store(momv, out_momentum, 0))
    parv[...] = parv[...] - outer_rate * (shift + momentum_decay * mom)
    stores.append(store(parv, out_params, 1))
    for c in stores:
        c.wait()


def body(
    tokens,
    expert_ids,
    router_weight,
    expert_weights,
    outer_params,
    outer_momentum,
    inner_drift,
    frag_index,
    out_grad,
):
    vmem = pl.BlockSpec(memory_space=pltpu.VMEM)
    anyw = pl.BlockSpec(memory_space=pl.ANY)
    dma = pltpu.SemaphoreType.DMA
    scratch = [
        pltpu.VMEM((TOK, D), BF16),
        pltpu.VMEM((TOK, D), BF16),
        pltpu.VMEM((D, 4 * HID), BF16),
        pltpu.VMEM((D, 2 * HID), BF16),
        pltpu.VMEM((FR, HID), F32),
        pltpu.VMEM((256, 256), BF16),
        pltpu.VMEM((2, ROWS * KC, LC), BF16),
        pltpu.VMEM((ROWS, D), BF16),
        pltpu.VMEM((ROWS, D), BF16),
        pltpu.VMEM((2, KC, ROWS, LC), BF16),
        pltpu.VMEM((2, ROWS * KC, LC), BF16),
        pltpu.VMEM((2, 2, 4 * BR, LC), BF16),
        pltpu.VMEM((2, 2, 8 * BR, LC), BF16),
        pltpu.VMEM((8, 2, BR, LC), BF16),
        pltpu.VMEM((FR, HID), F32),
        pltpu.VMEM((FR, HID), BF16),
        pltpu.VMEM((FR, HID), BF16),
        pltpu.VMEM((FR, HID), BF16),
        pltpu.VMEM((3, QR, HID), BF16),
        pltpu.VMEM((FR, HID), BF16),
        dma((6,)),
        dma((32,)),
        dma((8,)),
        dma((24,)),
        dma((3,)),
        dma((3,)),
        dma((8,)),
        dma((8,)),
        dma((16,)),
        dma((16,)),
        dma((8,)),
        dma((8,)),
        dma,
        dma,
        dma((3,)),
        dma((3,)),
        dma((3,)),
        dma((3,)),
    ]
    ids = expert_ids.T
    rows, pseudo = pl.pallas_call(
        kernel,
        out_shape=(
            jax.ShapeDtypeStruct((2, BR, LC), BF16),
            jax.ShapeDtypeStruct((FR, HID), BF16),
        ),
        in_specs=[anyw, vmem, vmem, anyw, anyw, vmem, anyw],
        out_specs=(vmem, vmem),
        scratch_shapes=scratch,
        compiler_params=pltpu.CompilerParams(
            collective_id=0, has_side_effects=True, vmem_limit_bytes=56 * 1024 * 1024
        ),
        cost_estimate=pl.CostEstimate(
            flops=4_000_000_000, bytes_accessed=12_000_000, transcendentals=100_000
        ),
    )(
        tokens,
        ids,
        router_weight,
        expert_weights,
        inner_drift,
        frag_index.reshape(1, 1),
        out_grad,
    )
    return pl.pallas_call(
        finish,
        out_shape=(
            jax.ShapeDtypeStruct((TOK, D), BF16),
            jax.ShapeDtypeStruct((TOK, D), BF16),
            jax.ShapeDtypeStruct((FR, HID), F32),
            jax.ShapeDtypeStruct((FR, HID), F32),
        ),
        in_specs=[vmem, anyw, anyw, anyw, anyw],
        out_specs=(anyw, anyw, anyw, anyw),
        scratch_shapes=[
            pltpu.VMEM((2, BR, LC), BF16),
            pltpu.VMEM((FR, HID), BF16),
            pltpu.VMEM((TOK, D), BF16),
            pltpu.VMEM((TOK, D), BF16),
            pltpu.VMEM((FR, HID), F32),
            pltpu.VMEM((FR, HID), F32),
            dma((8,)),
        ],
        compiler_params=pltpu.CompilerParams(vmem_limit_bytes=62 * 1024 * 1024),
    )(ids, rows, pseudo, outer_params, outer_momentum)


def solution(mesh):
    in_specs = (
        P(("replica", "fsdp"), None),
        P(("replica", "fsdp"), None),
        P("replica", None, None),
        P("replica", None, None, "fsdp"),
        P(None, "fsdp"),
        P(None, "fsdp"),
        P("replica", None, "fsdp"),
        P(),
        P(("replica", "fsdp"), None),
    )
    out_specs = (
        P(("replica", "fsdp"), None),
        P(("replica", "fsdp"), None),
        P(None, "fsdp"),
        P(None, "fsdp"),
    )
    return jax.shard_map(body, mesh=mesh, in_specs=in_specs, out_specs=out_specs, check_vma=False)
```

```python
import math

import jax
import jax.numpy as jnp
from jax import lax
from jax.experimental import pallas as pl
from jax.experimental.pallas import tpu as pltpu
from jax.sharding import PartitionSpec as P

D = 6144
FF = 8192
EXPERTS = 8
CAP = 3
FR = 768
TOK = 64
KC = 16
LC = D // KC
BR = CAP * KC
NX = 4
NY = 4
NZ = 2
HID = 128
ROWS = 96
QR = FR // 4
HR = QR // 2

inner_rate = 2.0
outer_rate = 0.7
momentum_decay = 0.9
scale_in = 1.0 / math.sqrt(D)
scale_hid = 1.0 / math.sqrt(FF)

MESH = pl.DeviceIdType.MESH
F32 = jnp.float32
BF16 = jnp.bfloat16
NT = (((1,), (1,)), ((), ()))
TN = (((0,), (0,)), ((), ()))


def dot(a, b, dims=(((1,), (0,)), ((), ()))):
    return lax.dot_general(a, b, dims, preferred_element_type=F32)


def iota(shape, dim):
    return lax.broadcasted_iota(jnp.int32, shape, dim)


def one(mask):
    return jnp.where(mask, 1.0, 0.0)


POS = (0, 1, 3, 2)
GROUP = ((0, 1), (1, 2), (3, 1))
MEMBERS = ((0,), (1, 3), (2,))


def row(slab, z, p):
    return ((slab * NZ + z) * 4 + POS[p]) * BR


def group_rows(slab, z, g):
    return pl.ds(((slab * NZ + z) * 4 + GROUP[g][0]) * BR, GROUP[g][1] * BR)


def id_rows(ids):
    id0, id1 = ids[0:1, :], ids[1:2, :]
    at = iota((16, TOK), 0)
    routed = one((id0 == 0) | (id1 == 0))
    other = (id0 + id1).astype(F32)
    return jnp.where(at == 0, routed, jnp.where(at == 1, other, 0.0)).astype(BF16)


def kernel(
    tokens,
    ids_hbm,
    router_hbm,
    weights,
    drift,
    frag_hbm,
    grads,
    out_rows,
    out_pseudo,
    ids,
    router,
    frag,
    tokv,
    grdv,
    wgu,
    wdn,
    drfv,
    perm,
    ag,
    xv,
    gv,
    yv,
    rb,
    t2,
    d2,
    e1,
    fq,
    fb,
    fs,
    fh,
    fr,
    ps,
    load_sem,
    n_send,
    n_recv,
    r_send,
    r_recv,
    w_send,
    w_recv,
    t2_send,
    t2_recv,
    d2_send,
    d2_recv,
    e1_send,
    e1_recv,
    f_send,
    f_recv,
    q_send,
    q_recv,
    p_send,
    p_recv,
):
    rep = lax.axis_index("replica")
    me = lax.axis_index("fsdp")
    core = me % 2
    py = (me // 2) % NY
    px = (me // (2 * NY)) % NX
    pz = me // (2 * NY * NX)
    first = 1 - core

    def dev(z, x, y, c):
        return {"fsdp": ((z * NX + x) * NY + y) * 2 + c}

    def at1(z, step):
        x = (px + first * step) % NX
        y = (py + core * step) % NY
        return dev((pz + z) % NZ, x, y, core)

    def at2(step):
        return dev(pz, (px + core * step) % NX, (py + first * step) % NY, core)

    up2, dn2 = at2(1), at2(3)
    sib = dev(pz, px, py, 1 - core)
    near = {(z, p): at1(z, p) for z in range(NZ) for p in range(4) if (z, p) != (0, 0)}
    reps = [{"replica": (rep + d) % 4} for d in (1, 2, 3)]

    def load(src, dst, i):
        c = pltpu.make_async_copy(src, dst, load_sem.at[i])
        c.start()
        return c

    load_ids = load(ids_hbm, ids, 6)
    load_rtr = load(router_hbm, router, 7)
    load_frag = load(frag_hbm, frag, 8)
    load_tok = load(tokens, tokv, 0)
    load_grd = load(grads, grdv, 1)

    barrier = pltpu.get_barrier_semaphore()
    peers = [up2, dn2, sib] + list(near.values()) + reps
    for p in peers:
        pl.semaphore_signal(barrier, inc=1, device_id=p, device_id_type=MESH)

    def send(src, dst, ssem, rsem, to):
        c = pltpu.make_async_remote_copy(
            src_ref=src, dst_ref=dst, send_sem=ssem, recv_sem=rsem,
            device_id=to, device_id_type=MESH,
        )
        c.start()
        return c

    def arrived(dst, rsem):
        pltpu.make_async_copy(dst, dst, rsem).wait()

    pending = []

    load_ids.wait()
    rows8 = id_rows(ids)
    wide = (TOK, KC * TOK)
    tiled = dot(rows8, one(iota(wide, 0) == iota(wide, 1) % TOK).astype(BF16))
    count = dot(rows8, one(iota(wide, 0) <= iota(wide, 1) % TOK).astype(BF16))
    sshape = (BR, KC * TOK)
    smask = (
        (tiled[0:1] > 0.5)
        & (count[0:1] - 1.0 == (iota(sshape, 0) // KC).astype(F32))
        & (iota(sshape, 0) % KC == iota(sshape, 1) // TOK)
    )
    select = one(smask).astype(BF16)
    other48 = jnp.sum(jnp.where(smask, tiled[1:2], 0.0), axis=1, keepdims=True)
    dshape = (BR, KC * EXPERTS)
    expert = iota(dshape, 1) % EXPERTS
    signs = jnp.where(
        iota(dshape, 0) % KC == iota(dshape, 1) // EXPERTS,
        one(expert == 0) - one(expert.astype(F32) == other48),
        0.0,
    ).astype(BF16)
    load_rtr.wait()
    load_frag.wait()
    rw = router[0].astype(F32)
    router2 = jnp.concatenate([rw[:, k * LC : (k + 1) * LC] for k in range(KC)], axis=0)
    differ = dot(signs, router2.astype(BF16))

    pshape = (256, 256)
    perm[...] = one(
        (iota(pshape, 0) // 16 == iota(pshape, 1) % 16)
        & (iota(pshape, 0) % 16 == iota(pshape, 1) // 16)
    ).astype(BF16)

    def fold(ref):
        stacked = jnp.concatenate([ref[:, k * LC : (k + 1) * LC] for k in range(KC)], axis=0)
        return dot(select, stacked)

    load_tok.wait()
    xsel = fold(tokv)
    ag[0, 0:BR, :] = xsel.astype(BF16)

    pl.semaphore_wait(barrier, len(peers))

    def piece(ref, i, slab, z, p):
        return ref.at[i, pl.ds(row(slab, z, p), BR), :]

    def group(ref, i, slab, z, g):
        return ref.at[i, group_rows(slab, z, g), :]

    def put(src, dst, ssem, rsem, to):
        pending.append(send(src, dst, ssem, rsem, to))

    far_last = [(1, 0), (0, 1), (0, 3), (1, 1), (1, 3), (0, 2), (1, 2)]

    def to_near(i):
        for z, p in far_last:
            q = (4 - p) % 4
            put(
                piece(ag, i, 0, 0, 0), piece(ag, i, 0, z, q),
                n_send.at[i, z * 4 + p], n_recv.at[i, z * 4 + q], near[z, p],
            )

    def to_ring(i, z, g):
        j = z * 3 + g
        src = group(ag, i, 0, z, g)
        put(src, group(ag, i, 3, z, g), r_send.at[i, 0, j], r_recv.at[i, 3, j], up2)
        put(src, group(ag, i, 1, z, g), r_send.at[i, 1, j], r_recv.at[i, 1, j], dn2)

    def near_to_ring(z, g):
        for i in range(2):
            for p in MEMBERS[g]:
                arrived(piece(ag, i, 0, z, p), n_recv.at[i, z * 4 + p])
            to_ring(i, z, g)

    def got_ring(i, slab, z, g):
        arrived(group(ag, i, slab, z, g), r_recv.at[i, slab, z * 3 + g])

    def relay(z, g):
        j = z * 3 + g
        for i in range(2):
            got_ring(i, 3, z, g)
            if z == 0:
                src = group(ag, i, 3, z, g)
                put(src, group(ag, i, 2, z, g), r_send.at[i, 2, j], r_recv.at[i, 2, j], up2)
            got_ring(i, 1, z, g)
            if z == 1:
                src = group(ag, i, 1, z, g)
                put(src, group(ag, i, 2, z, g), r_send.at[i, 2, j], r_recv.at[i, 2, j], dn2)

    def unfold(lo, hi):
        @pl.loop(lo, hi, unroll=True)
        def _(g):
            rows_at = pl.ds(pl.multiple_of(g * 16, 16), 16)
            for i, dst in ((0, xv), (1, gv)):
                v = ag[i, pl.ds(pl.multiple_of(g * 256, 256), 256), :]
                r = dot(perm[...], v).astype(BF16)
                for k in range(KC):
                    dst[rows_at, k * LC : (k + 1) * LC] = r[16 * k : 16 * k + 16]

    to_ring(0, 0, 0)
    to_near(0)
    logit = jnp.sum((xsel * differ).reshape(CAP, KC, LC), axis=(1, 2), keepdims=True)
    prob = jax.nn.sigmoid(jnp.broadcast_to(logit * scale_in, (CAP, KC, LC)).reshape(BR, LC))
    load_grd.wait()
    gsel = fold(grdv)
    ag[1, 0:BR, :] = (prob * gsel).astype(BF16)
    to_ring(1, 0, 0)
    to_near(1)

    loads = []
    for m, (dst, lo, far) in enumerate(((wgu, 0, 2 * HID), (wgu, HID, 3 * HID), (wdn, 0, HID))):
        src = weights.at[0, m]
        loads.append(load(src, dst.at[:, lo : lo + HID], 2 + m))
        put(src, dst.at[:, far : far + HID], w_send.at[m], w_recv.at[m], sib)
    loads.append(load(drift.at[0], drfv, 5))

    order = [(0, 0), (1, 0), (0, 1), (1, 1), (0, 2), (1, 2)]
    for z, g in order[1:]:
        near_to_ring(z, g)
    for z, g in order:
        relay(z, g)
    unfold(0, 3)
    for z, g in order:
        got_ring(0, 2, z, g)
        got_ring(1, 2, z, g)
    unfold(3, 6)

    for c in loads:
        c.wait()
    for m, (dst, far) in enumerate(((wgu, 2 * HID), (wgu, 3 * HID), (wdn, HID))):
        arrived(dst.at[:, far : far + HID], w_recv.at[m])
    gu = dot(xv[...], wgu[...]) * scale_in
    gate = jnp.concatenate([gu[:, 0:HID], gu[:, 2 * HID : 3 * HID]], axis=1)
    up = jnp.concatenate([gu[:, HID : 2 * HID], gu[:, 3 * HID :]], axis=1)
    sigma = jax.nn.sigmoid(gate)
    active = gate * sigma
    hidden = (active * up).astype(BF16)
    d_hidden = dot(gv[...], wdn[...]) * scale_hid
    d_gate = (d_hidden * up * (sigma + gate * sigma * (1.0 - sigma))).astype(BF16)
    d_up = (d_hidden * active).astype(BF16)
    d_gu = jnp.concatenate(
        [d_gate[:, :HID], d_up[:, :HID], d_gate[:, HID:], d_up[:, HID:]], axis=1
    )

    which = frag[...]
    per = D // FR
    masks = [one((which >= m * per) & (which < (m + 1) * per)) for m in range(3)]
    left = jnp.zeros((ROWS, FR), BF16)
    for src, off in ((xv, 1.0 - masks[2]), (gv, masks[2])):
        for c in range(per):
            here = one((which == c) | (which == per + c) | (which == 2 * per + c))
            left = left + src[:, c * FR : (c + 1) * FR] * (off * here).astype(BF16)
    right = (
        d_gate * masks[0].astype(BF16)
        + d_up * masks[1].astype(BF16)
        + hidden * masks[2].astype(BF16)
    )
    factor = inner_rate * (scale_in * (1.0 - masks[2]) + scale_hid * masks[2])
    partial = dot(left, right, TN) * factor
    fb[...] = partial[:, HID:].astype(BF16)
    put(fb, fs, f_send, f_recv, sib)
    fq[...] = partial[:, :HID] - drfv[...]

    def back(i, rows_at, w, scale):
        for k in range(KC):
            part = dot(rows_at, w[k * LC : (k + 1) * LC, :], NT)
            yv[i, k] = (part * scale).astype(BF16)

    def refold(i, lo, hi):
        @pl.loop(lo, hi, unroll=True)
        def _(g):
            v = yv[i, :, pl.ds(pl.multiple_of(g * 16, 16), 16), :].reshape(256, LC)
            rb[i, pl.ds(pl.multiple_of(g * 256, 256), 256), :] = dot(perm[...], v).astype(BF16)

    def transit(i, way, g):
        at = pl.ds(GROUP[g][0] * BR, GROUP[g][1] * BR)
        return t2.at[i, way, at, :]

    def landing(i, way, z, g):
        return d2.at[i, way, group_rows(0, z, g), :]

    def send_transit(i, way, g, to):
        put(
            group(rb, i, 2, way, g), transit(i, way, g),
            t2_send.at[i, way, g], t2_recv.at[i, way, g], to,
        )

    def send_landing(i, way, slab, z, g, to):
        j = z * 3 + g
        put(
            group(rb, i, slab, z, g), landing(i, way, z, g),
            d2_send.at[i, way, j], d2_recv.at[i, way, j], to,
        )

    def add_into(i, at, *others):
        v = rb[i, at, :].astype(F32)
        for other in others:
            v = v + other[...].astype(F32)
        rb[i, at, :] = v.astype(BF16)

    def scatter_start(i):
        refold(i, 3, 6)
        for g in (2, 1, 0):
            send_transit(i, 0, g, up2)
            send_transit(i, 1, g, dn2)
        refold(i, 0, 3)

    def scatter_direct(i, g):
        send_landing(i, 0, 1, 1, g, up2)
        send_landing(i, 1, 3, 0, g, dn2)

    def scatter_relay(i, g):
        arrived(transit(i, 0, g), t2_recv.at[i, 0, g])
        add_into(i, group_rows(1, 0, g), transit(i, 0, g))
        send_landing(i, 0, 1, 0, g, up2)
        arrived(transit(i, 1, g), t2_recv.at[i, 1, g])
        add_into(i, group_rows(3, 1, g), transit(i, 1, g))
        send_landing(i, 1, 3, 1, g, dn2)

    def scatter_near(i, g):
        for z in (1, 0):
            for way in range(2):
                arrived(landing(i, way, z, g), d2_recv.at[i, way, z * 3 + g])
            add_into(i, group_rows(0, z, g), landing(i, 0, z, g), landing(i, 1, z, g))
            for p in MEMBERS[g]:
                if (z, p) != (0, 0):
                    j = z * 4 + (4 - p) % 4
                    put(
                        piece(rb, i, 0, z, p), e1.at[i, j],
                        e1_send.at[i, z * 4 + p], e1_recv.at[i, j], near[z, p],
                    )

    def scatter_end(i):
        v = rb[i, 0:BR, :].astype(F32)
        for z, p in far_last:
            j = z * 4 + p
            arrived(e1.at[i, j], e1_recv.at[i, j])
            v = v + e1[i, j].astype(F32)
        return v

    back(0, hidden, wdn, scale_hid)
    arrived(fs, f_recv)
    fq[...] = fq[...] + fs[...].astype(F32)
    fh[...] = fq[...].astype(BF16)

    def half(quarter, h):
        return pl.ds(pl.multiple_of(quarter * QR + h * HR, 32), HR)

    for h in range(2):
        for d in (1, 0, 2):
            at = half((rep + d + 1) % 4, h)
            put(fh.at[at, :], fr.at[d, h], q_send.at[d, h], q_recv.at[d, h], reps[d])

    def sum_quarter(h):
        own = half(rep, h)
        total = fq[own, :]
        for d in range(3):
            arrived(fr.at[d, h], q_recv.at[d, h])
            total = total + fr[d, h].astype(F32)
        ps[own, :] = (total * 0.25).astype(BF16)
        for d in (1, 0, 2):
            put(ps.at[own, :], ps.at[own, :], p_send.at[d, h], p_recv.at[d, h], reps[d])

    scatter_start(0)
    for g in (2, 1, 0):
        scatter_direct(0, g)
    back(1, d_gu, wgu, scale_in)
    scatter_start(1)
    for g in (2, 1, 0):
        scatter_relay(0, g)
    scatter_direct(1, 2)
    scatter_relay(1, 2)
    scatter_direct(1, 1)
    scatter_relay(1, 1)
    scatter_direct(1, 0)
    scatter_relay(1, 0)
    sum_quarter(0)
    scatter_near(0, 2)
    scatter_near(0, 1)
    sum_quarter(1)
    scatter_near(0, 0)
    for g in (2, 1, 0):
        scatter_near(1, g)
    y = scatter_end(0)

    d_prob = jnp.sum((gsel * y).reshape(CAP, KC, LC), axis=(1, 2), keepdims=True)
    d_prob = jnp.broadcast_to(d_prob, (CAP, KC, LC)).reshape(BR, LC)
    d_logit = d_prob * prob * (1.0 - prob)
    out_rows[0] = (prob * y).astype(BF16)
    dx = scatter_end(1)
    out_rows[1] = (dx + (d_logit * scale_in) * differ).astype(BF16)

    for h in range(2):
        for d in range(3):
            at = half((rep + 3 - d) % 4, h)
            arrived(ps.at[at, :], p_recv.at[d, h])
    out_pseudo[...] = ps[...]

    for c in pending:
        c.wait_send()


def finish(
    ids, rows, pseudo, params, momentum,
    out_mixed, out_grad, out_params, out_momentum,
    mixv, grdv, parv, momv, sem,
):
    def store(src, dst, i):
        c = pltpu.make_async_copy(src, dst, sem.at[i])
        c.start()
        return c


    rows8 = id_rows(ids)
    tri = one(iota((TOK, TOK), 0) >= iota((TOK, TOK), 1)).astype(BF16)
    eye = one(iota((TOK, TOK), 0) == iota((TOK, TOK), 1)).astype(BF16)
    slot = dot(tri, rows8, NT)[:, 0:1] - 1.0
    routed = dot(eye, rows8, NT)[:, 0:1]
    shape = (TOK, BR)
    mine = (slot == (iota(shape, 1) // KC).astype(F32)) & (routed > 0.5)
    spread = jnp.concatenate(
        [one(mine & (iota(shape, 1) % KC == k)).astype(BF16) for k in range(KC)], axis=0
    )
    stores = []
    for src, buf, dst in ((0, mixv, out_mixed), (1, grdv, out_grad)):
        placed = dot(spread, rows[src]).astype(BF16)
        for k in range(KC):
            buf[:, k * LC : (k + 1) * LC] = placed[k * TOK : (k + 1) * TOK]
        stores.append(store(buf, dst, 2 + src))
    shift = pseudo[...].astype(F32)
    mom = momentum_decay * momentum[...] + shift
    momv[...] = mom
    stores.append(store(momv, out_momentum, 0))
    parv[...] = params[...] - outer_rate * (shift + momentum_decay * mom)
    stores.append(store(parv, out_params, 1))
    for c in stores:
        c.wait()


def body(
    tokens,
    expert_ids,
    router_weight,
    expert_weights,
    outer_params,
    outer_momentum,
    inner_drift,
    frag_index,
    out_grad,
):
    vmem = pl.BlockSpec(memory_space=pltpu.VMEM)
    anyw = pl.BlockSpec(memory_space=pl.ANY)
    dma = pltpu.SemaphoreType.DMA
    scratch = [
        pltpu.VMEM((2, TOK), jnp.int32),
        pltpu.VMEM((1, EXPERTS, D), BF16),
        pltpu.VMEM((1, 1), jnp.int32),
        pltpu.VMEM((TOK, D), BF16),
        pltpu.VMEM((TOK, D), BF16),
        pltpu.VMEM((D, 4 * HID), BF16),
        pltpu.VMEM((D, 2 * HID), BF16),
        pltpu.VMEM((FR, HID), F32),
        pltpu.VMEM((256, 256), BF16),
        pltpu.VMEM((2, ROWS * KC, LC), BF16),
        pltpu.VMEM((ROWS, D), BF16),
        pltpu.VMEM((ROWS, D), BF16),
        pltpu.VMEM((2, KC, ROWS, LC), BF16),
        pltpu.VMEM((2, ROWS * KC, LC), BF16),
        pltpu.VMEM((2, 2, 4 * BR, LC), BF16),
        pltpu.VMEM((2, 2, 8 * BR, LC), BF16),
        pltpu.VMEM((2, 8, BR, LC), BF16),
        pltpu.VMEM((FR, HID), F32),
        pltpu.VMEM((FR, HID), BF16),
        pltpu.VMEM((FR, HID), BF16),
        pltpu.VMEM((FR, HID), BF16),
        pltpu.VMEM((3, 2, HR, HID), BF16),
        pltpu.VMEM((FR, HID), BF16),
        dma((9,)),
        dma((2, 8)),
        dma((2, 8)),
        dma((2, 3, 6)),
        dma((2, 4, 6)),
        dma((3,)),
        dma((3,)),
        dma((2, 2, 3)),
        dma((2, 2, 3)),
        dma((2, 2, 6)),
        dma((2, 2, 6)),
        dma((2, 8)),
        dma((2, 8)),
        dma,
        dma,
        dma((3, 2)),
        dma((3, 2)),
        dma((3, 2)),
        dma((3, 2)),
    ]
    ids = expert_ids.T
    rows, pseudo = pl.pallas_call(
        kernel,
        out_shape=(
            pltpu.VMEM((2, BR, LC), BF16),
            pltpu.VMEM((FR, HID), BF16),
        ),
        in_specs=[anyw] * 7,
        out_specs=(vmem, vmem),
        scratch_shapes=scratch,
        compiler_params=pltpu.CompilerParams(
            collective_id=0, has_side_effects=True, vmem_limit_bytes=56 * 1024 * 1024
        ),
        cost_estimate=pl.CostEstimate(
            flops=4_000_000_000, bytes_accessed=12_000_000, transcendentals=100_000
        ),
    )(
        tokens,
        ids,
        router_weight,
        expert_weights,
        inner_drift,
        frag_index.reshape(1, 1),
        out_grad,
    )
    return pl.pallas_call(
        finish,
        out_shape=(
            jax.ShapeDtypeStruct((TOK, D), BF16),
            jax.ShapeDtypeStruct((TOK, D), BF16),
            jax.ShapeDtypeStruct((FR, HID), F32),
            jax.ShapeDtypeStruct((FR, HID), F32),
        ),
        in_specs=[vmem] * 5,
        out_specs=(anyw, anyw, anyw, anyw),
        scratch_shapes=[
            pltpu.VMEM((TOK, D), BF16),
            pltpu.VMEM((TOK, D), BF16),
            pltpu.VMEM((FR, HID), F32),
            pltpu.VMEM((FR, HID), F32),
            dma((4,)),
        ],
        compiler_params=pltpu.CompilerParams(vmem_limit_bytes=16 * 1024 * 1024),
    )(ids, rows, pseudo, outer_params, outer_momentum)


def solution(mesh):
    in_specs = (
        P(("replica", "fsdp"), None),
        P(("replica", "fsdp"), None),
        P("replica", None, None),
        P("replica", None, None, "fsdp"),
        P(None, "fsdp"),
        P(None, "fsdp"),
        P("replica", None, "fsdp"),
        P(),
        P(("replica", "fsdp"), None),
    )
    out_specs = (
        P(("replica", "fsdp"), None),
        P(("replica", "fsdp"), None),
        P(None, "fsdp"),
        P(None, "fsdp"),
    )
    return jax.shard_map(body, mesh=mesh, in_specs=in_specs, out_specs=out_specs, check_vma=False)
```

```python
import math

import jax
import jax.numpy as jnp
from jax import lax
from jax.experimental import pallas as pl
from jax.experimental.pallas import tpu as pltpu
from jax.sharding import PartitionSpec as P

D = 6144
FF = 8192
EXPERTS = 8
CAP = 3
FR = 768
TOK = 64
KC = 16
LC = D // KC
BR = CAP * KC
NX = 4
NY = 4
NZ = 2
HID = 128
ROWS = 96
QR = FR // 4
HR = QR // 2

inner_rate = 2.0
outer_rate = 0.7
momentum_decay = 0.9
scale_in = 1.0 / math.sqrt(D)
scale_hid = 1.0 / math.sqrt(FF)

MESH = pl.DeviceIdType.MESH
F32 = jnp.float32
BF16 = jnp.bfloat16
NT = (((1,), (1,)), ((), ()))
TN = (((0,), (0,)), ((), ()))


def dot(a, b, dims=(((1,), (0,)), ((), ()))):
    return lax.dot_general(a, b, dims, preferred_element_type=F32)


def iota(shape, dim):
    return lax.broadcasted_iota(jnp.int32, shape, dim)


def one(mask):
    return jnp.where(mask, 1.0, 0.0)


POS = (0, 1, 3, 2)
GROUP = ((0, 1), (1, 2), (3, 1))
MEMBERS = ((0,), (1, 3), (2,))


def row(slab, z, p):
    return ((slab * NZ + z) * 4 + POS[p]) * BR


def group_rows(slab, z, g):
    return pl.ds(((slab * NZ + z) * 4 + GROUP[g][0]) * BR, GROUP[g][1] * BR)


def id_rows(ids):
    id0, id1 = ids[0:1, :], ids[1:2, :]
    at = iota((16, TOK), 0)
    routed = one((id0 == 0) | (id1 == 0))
    other = (id0 + id1).astype(F32)
    return jnp.where(at == 0, routed, jnp.where(at == 1, other, 0.0)).astype(BF16)


def kernel(
    tokens,
    ids_hbm,
    router_hbm,
    weights,
    drift,
    frag_hbm,
    grads,
    out_rows,
    out_pseudo,
    ids,
    router,
    frag,
    tokv,
    grdv,
    wgu,
    wdn,
    drfv,
    perm,
    ag,
    xv,
    gv,
    yv,
    rb,
    t2,
    d2,
    e1,
    fq,
    fb,
    fs,
    fh,
    fr,
    ps,
    load_sem,
    n_send,
    n_recv,
    r_send,
    r_recv,
    w_send,
    w_recv,
    t2_send,
    t2_recv,
    d2_send,
    d2_recv,
    e1_send,
    e1_recv,
    f_send,
    f_recv,
    q_send,
    q_recv,
    p_send,
    p_recv,
):
    rep = lax.axis_index("replica")
    me = lax.axis_index("fsdp")
    core = me % 2
    py = (me // 2) % NY
    px = (me // (2 * NY)) % NX
    pz = me // (2 * NY * NX)
    first = 1 - core

    def dev(z, x, y, c):
        return {"fsdp": ((z * NX + x) * NY + y) * 2 + c}

    def at1(z, step):
        x = (px + first * step) % NX
        y = (py + core * step) % NY
        return dev((pz + z) % NZ, x, y, core)

    def at2(step):
        return dev(pz, (px + core * step) % NX, (py + first * step) % NY, core)

    up2, dn2 = at2(1), at2(3)
    sib = dev(pz, px, py, 1 - core)
    near = {(z, p): at1(z, p) for z in range(NZ) for p in range(4) if (z, p) != (0, 0)}
    reps = [{"replica": (rep + d) % 4} for d in (1, 2, 3)]

    def load(src, dst, i):
        c = pltpu.make_async_copy(src, dst, load_sem.at[i])
        c.start()
        return c

    load_ids = load(ids_hbm, ids, 6)
    load_rtr = load(router_hbm, router, 7)
    load_frag = load(frag_hbm, frag, 8)
    load_tok = load(tokens, tokv, 0)
    load_grd = load(grads, grdv, 1)

    barrier = pltpu.get_barrier_semaphore()
    peers = [up2, dn2, sib] + list(near.values()) + reps
    for p in peers:
        pl.semaphore_signal(barrier, inc=1, device_id=p, device_id_type=MESH)

    def send(src, dst, ssem, rsem, to):
        c = pltpu.make_async_remote_copy(
            src_ref=src, dst_ref=dst, send_sem=ssem, recv_sem=rsem,
            device_id=to, device_id_type=MESH,
        )
        c.start()
        return c

    def arrived(dst, rsem):
        pltpu.make_async_copy(dst, dst, rsem).wait()

    pending = []

    load_ids.wait()
    rows8 = id_rows(ids)
    wide = (TOK, KC * TOK)
    tiled = dot(rows8, one(iota(wide, 0) == iota(wide, 1) % TOK).astype(BF16))
    count = dot(rows8, one(iota(wide, 0) <= iota(wide, 1) % TOK).astype(BF16))
    sshape = (BR, KC * TOK)
    smask = (
        (tiled[0:1] > 0.5)
        & (count[0:1] - 1.0 == (iota(sshape, 0) // KC).astype(F32))
        & (iota(sshape, 0) % KC == iota(sshape, 1) // TOK)
    )
    select = one(smask).astype(BF16)
    other48 = jnp.sum(jnp.where(smask, tiled[1:2], 0.0), axis=1, keepdims=True)
    dshape = (BR, KC * EXPERTS)
    expert = iota(dshape, 1) % EXPERTS
    signs = jnp.where(
        iota(dshape, 0) % KC == iota(dshape, 1) // EXPERTS,
        one(expert == 0) - one(expert.astype(F32) == other48),
        0.0,
    ).astype(BF16)
    load_rtr.wait()
    load_frag.wait()
    rw = router[0].astype(F32)
    router2 = jnp.concatenate([rw[:, k * LC : (k + 1) * LC] for k in range(KC)], axis=0)
    differ = dot(signs, router2.astype(BF16))

    pshape = (256, 256)
    perm[...] = one(
        (iota(pshape, 0) // 16 == iota(pshape, 1) % 16)
        & (iota(pshape, 0) % 16 == iota(pshape, 1) // 16)
    ).astype(BF16)

    def fold(ref):
        stacked = jnp.concatenate([ref[:, k * LC : (k + 1) * LC] for k in range(KC)], axis=0)
        return dot(select, stacked)

    load_tok.wait()
    xsel = fold(tokv)
    ag[0, 0:BR, :] = xsel.astype(BF16)

    pl.semaphore_wait(barrier, len(peers))

    def piece(ref, i, slab, z, p):
        return ref.at[i, pl.ds(row(slab, z, p), BR), :]

    def group(ref, i, slab, z, g):
        return ref.at[i, group_rows(slab, z, g), :]

    def put(src, dst, ssem, rsem, to):
        pending.append(send(src, dst, ssem, rsem, to))

    far_last = [(1, 0), (0, 1), (0, 3), (1, 1), (1, 3), (0, 2), (1, 2)]

    def to_near(i):
        for z, p in far_last:
            q = (4 - p) % 4
            put(
                piece(ag, i, 0, 0, 0), piece(ag, i, 0, z, q),
                n_send.at[i, z * 4 + p], n_recv.at[i, z * 4 + q], near[z, p],
            )

    def to_ring(i, z, g):
        j = z * 3 + g
        src = group(ag, i, 0, z, g)
        put(src, group(ag, i, 3, z, g), r_send.at[i, 0, j], r_recv.at[i, 3, j], up2)
        put(src, group(ag, i, 1, z, g), r_send.at[i, 1, j], r_recv.at[i, 1, j], dn2)

    def near_to_ring(i, z, g):
        for p in MEMBERS[g]:
            arrived(piece(ag, i, 0, z, p), n_recv.at[i, z * 4 + p])
        to_ring(i, z, g)

    def got_ring(i, slab, z, g):
        arrived(group(ag, i, slab, z, g), r_recv.at[i, slab, z * 3 + g])

    def relay(i, z, g):
        j = z * 3 + g
        got_ring(i, 3, z, g)
        if z == 0:
            src = group(ag, i, 3, z, g)
            put(src, group(ag, i, 2, z, g), r_send.at[i, 2, j], r_recv.at[i, 2, j], up2)
        got_ring(i, 1, z, g)
        if z == 1:
            src = group(ag, i, 1, z, g)
            put(src, group(ag, i, 2, z, g), r_send.at[i, 2, j], r_recv.at[i, 2, j], dn2)

    def unfold(i, dst, lo, hi):
        @pl.loop(lo, hi, unroll=True)
        def _(g):
            rows_at = pl.ds(pl.multiple_of(g * 16, 16), 16)
            v = ag[i, pl.ds(pl.multiple_of(g * 256, 256), 256), :]
            r = dot(perm[...], v).astype(BF16)
            for k in range(KC):
                dst[rows_at, k * LC : (k + 1) * LC] = r[16 * k : 16 * k + 16]

    to_ring(0, 0, 0)
    to_near(0)
    logit = jnp.sum((xsel * differ).reshape(CAP, KC, LC), axis=(1, 2), keepdims=True)
    prob = jax.nn.sigmoid(jnp.broadcast_to(logit * scale_in, (CAP, KC, LC)).reshape(BR, LC))
    load_grd.wait()
    gsel = fold(grdv)
    ag[1, 0:BR, :] = (prob * gsel).astype(BF16)
    to_ring(1, 0, 0)
    to_near(1)

    loads = []
    for m, (dst, lo, far) in enumerate(((wgu, 0, 2 * HID), (wgu, HID, 3 * HID), (wdn, 0, HID))):
        src = weights.at[0, m]
        loads.append(load(src, dst.at[:, lo : lo + HID], 2 + m))
        put(src, dst.at[:, far : far + HID], w_send.at[m], w_recv.at[m], sib)
    loads.append(load(drift.at[0], drfv, 5))

    order = [(0, 0), (1, 0), (0, 1), (1, 1), (0, 2), (1, 2)]
    for j in range(1, 10):
        if j < 6:
            near_to_ring(0, *order[j])
        if j > 4:
            near_to_ring(1, *order[j - 4])
    for j in range(10):
        if j < 6:
            relay(0, *order[j])
        if j >= 4:
            relay(1, *order[j - 4])
    unfold(0, xv, 0, 3)
    unfold(1, gv, 0, 3)
    for z, g in order:
        got_ring(0, 2, z, g)
    unfold(0, xv, 3, 6)

    for c in loads:
        c.wait()
    for m, (dst, far) in enumerate(((wgu, 2 * HID), (wgu, 3 * HID), (wdn, HID))):
        arrived(dst.at[:, far : far + HID], w_recv.at[m])
    gu = dot(xv[...], wgu[...]) * scale_in
    gate = jnp.concatenate([gu[:, 0:HID], gu[:, 2 * HID : 3 * HID]], axis=1)
    up = jnp.concatenate([gu[:, HID : 2 * HID], gu[:, 3 * HID :]], axis=1)
    sigma = jax.nn.sigmoid(gate)
    active = gate * sigma
    hidden = (active * up).astype(BF16)
    def back(i, rows_at, w, scale):
        for k in range(KC):
            part = dot(rows_at, w[k * LC : (k + 1) * LC, :], NT)
            for c in range(LC // 128):
                lanes = slice(c * 128, (c + 1) * 128)
                yv[i, c, pl.ds(k, ROWS, stride=KC), :] = part[:, lanes] * scale

    def refold(i, lo, hi):
        at = pl.ds(lo * 256, (hi - lo) * 256)
        for c in range(LC // 128):
            rb[i, at, c * 128 : (c + 1) * 128] = yv[i, c, at, :].astype(BF16)

    def transit(i, way, g):
        at = pl.ds(GROUP[g][0] * BR, GROUP[g][1] * BR)
        return t2.at[i, way, at, :]

    def landing(i, way, z, g):
        return d2.at[i, way, group_rows(0, z, g), :]

    def send_transit(i, way, g, to):
        put(
            group(rb, i, 2, way, g), transit(i, way, g),
            t2_send.at[i, way, g], t2_recv.at[i, way, g], to,
        )

    def send_landing(i, way, slab, z, g, to):
        j = z * 3 + g
        put(
            group(rb, i, slab, z, g), landing(i, way, z, g),
            d2_send.at[i, way, j], d2_recv.at[i, way, j], to,
        )

    def add_into(i, at, *others):
        v = rb[i, at, :].astype(F32)
        for other in others:
            v = v + other[...].astype(F32)
        rb[i, at, :] = v.astype(BF16)

    def scatter_start(i):
        refold(i, 3, 6)
        for g in (2, 1, 0):
            send_transit(i, 0, g, up2)
            send_transit(i, 1, g, dn2)
        refold(i, 0, 3)

    def scatter_direct(i, g):
        send_landing(i, 0, 1, 1, g, up2)
        send_landing(i, 1, 3, 0, g, dn2)

    def scatter_relay(i, g):
        arrived(transit(i, 0, g), t2_recv.at[i, 0, g])
        add_into(i, group_rows(1, 0, g), transit(i, 0, g))
        send_landing(i, 0, 1, 0, g, up2)
        arrived(transit(i, 1, g), t2_recv.at[i, 1, g])
        add_into(i, group_rows(3, 1, g), transit(i, 1, g))
        send_landing(i, 1, 3, 1, g, dn2)

    def scatter_near(i, g):
        for z in (1, 0):
            for way in range(2):
                arrived(landing(i, way, z, g), d2_recv.at[i, way, z * 3 + g])
            add_into(i, group_rows(0, z, g), landing(i, 0, z, g), landing(i, 1, z, g))
            for p in MEMBERS[g]:
                if (z, p) != (0, 0):
                    j = z * 4 + (4 - p) % 4
                    put(
                        piece(rb, i, 0, z, p), e1.at[i, j],
                        e1_send.at[i, z * 4 + p], e1_recv.at[i, j], near[z, p],
                    )

    def scatter_end(i):
        v = rb[i, 0:BR, :].astype(F32)
        for z, p in far_last:
            j = z * 4 + p
            arrived(e1.at[i, j], e1_recv.at[i, j])
            v = v + e1[i, j].astype(F32)
        return v

    back(0, hidden, wdn, scale_hid)
    scatter_start(0)
    for g in (2, 1, 0):
        scatter_direct(0, g)
    for z, g in order:
        got_ring(1, 2, z, g)
    unfold(1, gv, 3, 6)
    d_hidden = dot(gv[...], wdn[...]) * scale_hid
    d_gate = (d_hidden * up * (sigma + gate * sigma * (1.0 - sigma))).astype(BF16)
    d_up = (d_hidden * active).astype(BF16)
    d_gu = jnp.concatenate(
        [d_gate[:, :HID], d_up[:, :HID], d_gate[:, HID:], d_up[:, HID:]], axis=1
    )

    which = frag[...]
    per = D // FR
    masks = [one((which >= m * per) & (which < (m + 1) * per)) for m in range(3)]
    left = jnp.zeros((ROWS, FR), BF16)
    for src, off in ((xv, 1.0 - masks[2]), (gv, masks[2])):
        for c in range(per):
            here = one((which == c) | (which == per + c) | (which == 2 * per + c))
            left = left + src[:, c * FR : (c + 1) * FR] * (off * here).astype(BF16)
    right = (
        d_gate * masks[0].astype(BF16)
        + d_up * masks[1].astype(BF16)
        + hidden * masks[2].astype(BF16)
    )
    factor = inner_rate * (scale_in * (1.0 - masks[2]) + scale_hid * masks[2])
    partial = dot(left, right, TN) * factor
    fb[...] = partial[:, HID:].astype(BF16)
    put(fb, fs, f_send, f_recv, sib)
    fq[...] = partial[:, :HID] - drfv[...]

    back(1, d_gu, wgu, scale_in)
    arrived(fs, f_recv)
    fq[...] = fq[...] + fs[...].astype(F32)
    fh[...] = fq[...].astype(BF16)

    def half(quarter, h):
        return pl.ds(pl.multiple_of(quarter * QR + h * HR, 32), HR)

    for h in range(2):
        for d in (1, 0, 2):
            at = half((rep + d + 1) % 4, h)
            put(fh.at[at, :], fr.at[d, h], q_send.at[d, h], q_recv.at[d, h], reps[d])

    def sum_quarter(h):
        own = half(rep, h)
        total = fq[own, :]
        for d in range(3):
            arrived(fr.at[d, h], q_recv.at[d, h])
            total = total + fr[d, h].astype(F32)
        ps[own, :] = (total * 0.25).astype(BF16)
        for d in (1, 0, 2):
            put(ps.at[own, :], ps.at[own, :], p_send.at[d, h], p_recv.at[d, h], reps[d])

    scatter_start(1)
    scatter_relay(0, 2)
    scatter_relay(0, 1)
    scatter_relay(0, 0)
    scatter_direct(1, 2)
    scatter_direct(1, 1)
    scatter_relay(1, 2)
    scatter_near(0, 2)
    scatter_direct(1, 0)
    scatter_relay(1, 1)
    scatter_near(0, 1)
    scatter_relay(1, 0)
    scatter_near(0, 0)
    sum_quarter(0)
    sum_quarter(1)
    scatter_near(1, 2)
    scatter_near(1, 1)
    scatter_near(1, 0)
    y = scatter_end(0)

    d_prob = jnp.sum((gsel * y).reshape(CAP, KC, LC), axis=(1, 2), keepdims=True)
    d_prob = jnp.broadcast_to(d_prob, (CAP, KC, LC)).reshape(BR, LC)
    d_logit = d_prob * prob * (1.0 - prob)
    out_rows[0] = (prob * y).astype(BF16)
    dx = scatter_end(1)
    out_rows[1] = (dx + (d_logit * scale_in) * differ).astype(BF16)

    for h in range(2):
        for d in range(3):
            at = half((rep + 3 - d) % 4, h)
            arrived(ps.at[at, :], p_recv.at[d, h])
    out_pseudo[...] = ps[...]

    for c in pending:
        c.wait_send()


def finish(
    ids, rows, pseudo, params, momentum,
    out_mixed, out_grad, out_params, out_momentum,
    mixv, grdv, parv, momv, sem,
):
    def store(src, dst, i):
        c = pltpu.make_async_copy(src, dst, sem.at[i])
        c.start()
        return c


    rows8 = id_rows(ids)
    tri = one(iota((TOK, TOK), 0) >= iota((TOK, TOK), 1)).astype(BF16)
    eye = one(iota((TOK, TOK), 0) == iota((TOK, TOK), 1)).astype(BF16)
    slot = dot(tri, rows8, NT)[:, 0:1] - 1.0
    routed = dot(eye, rows8, NT)[:, 0:1]
    shape = (TOK, BR)
    mine = (slot == (iota(shape, 1) // KC).astype(F32)) & (routed > 0.5)
    spread = jnp.concatenate(
        [one(mine & (iota(shape, 1) % KC == k)).astype(BF16) for k in range(KC)], axis=0
    )
    stores = []
    for src, buf, dst in ((0, mixv, out_mixed), (1, grdv, out_grad)):
        placed = dot(spread, rows[src]).astype(BF16)
        for k in range(KC):
            buf[:, k * LC : (k + 1) * LC] = placed[k * TOK : (k + 1) * TOK]
        stores.append(store(buf, dst, 2 + src))
    shift = pseudo[...].astype(F32)
    mom = momentum_decay * momentum[...] + shift
    momv[...] = mom
    stores.append(store(momv, out_momentum, 0))
    parv[...] = params[...] - outer_rate * (shift + momentum_decay * mom)
    stores.append(store(parv, out_params, 1))
    for c in stores:
        c.wait()


def body(
    tokens,
    expert_ids,
    router_weight,
    expert_weights,
    outer_params,
    outer_momentum,
    inner_drift,
    frag_index,
    out_grad,
):
    vmem = pl.BlockSpec(memory_space=pltpu.VMEM)
    anyw = pl.BlockSpec(memory_space=pl.ANY)
    dma = pltpu.SemaphoreType.DMA
    scratch = [
        pltpu.VMEM((2, TOK), jnp.int32),
        pltpu.VMEM((1, EXPERTS, D), BF16),
        pltpu.VMEM((1, 1), jnp.int32),
        pltpu.VMEM((TOK, D), BF16),
        pltpu.VMEM((TOK, D), BF16),
        pltpu.VMEM((D, 4 * HID), BF16),
        pltpu.VMEM((D, 2 * HID), BF16),
        pltpu.VMEM((FR, HID), F32),
        pltpu.VMEM((256, 256), BF16),
        pltpu.VMEM((2, ROWS * KC, LC), BF16),
        pltpu.VMEM((ROWS, D), BF16),
        pltpu.VMEM((ROWS, D), BF16),
        pltpu.VMEM((2, LC // 128, ROWS * KC, 128), F32),
        pltpu.VMEM((2, ROWS * KC, LC), BF16),
        pltpu.VMEM((2, 2, 4 * BR, LC), BF16),
        pltpu.VMEM((2, 2, 8 * BR, LC), BF16),
        pltpu.VMEM((2, 8, BR, LC), BF16),
        pltpu.VMEM((FR, HID), F32),
        pltpu.VMEM((FR, HID), BF16),
        pltpu.VMEM((FR, HID), BF16),
        pltpu.VMEM((FR, HID), BF16),
        pltpu.VMEM((3, 2, HR, HID), BF16),
        pltpu.VMEM((FR, HID), BF16),
        dma((9,)),
        dma((2, 8)),
        dma((2, 8)),
        dma((2, 3, 6)),
        dma((2, 4, 6)),
        dma((3,)),
        dma((3,)),
        dma((2, 2, 3)),
        dma((2, 2, 3)),
        dma((2, 2, 6)),
        dma((2, 2, 6)),
        dma((2, 8)),
        dma((2, 8)),
        dma,
        dma,
        dma((3, 2)),
        dma((3, 2)),
        dma((3, 2)),
        dma((3, 2)),
    ]
    ids = expert_ids.T
    rows, pseudo = pl.pallas_call(
        kernel,
        out_shape=(
            pltpu.VMEM((2, BR, LC), BF16),
            pltpu.VMEM((FR, HID), BF16),
        ),
        in_specs=[anyw] * 7,
        out_specs=(vmem, vmem),
        scratch_shapes=scratch,
        compiler_params=pltpu.CompilerParams(
            collective_id=0, has_side_effects=True, vmem_limit_bytes=56 * 1024 * 1024
        ),
        cost_estimate=pl.CostEstimate(
            flops=4_000_000_000, bytes_accessed=12_000_000, transcendentals=100_000
        ),
    )(
        tokens,
        ids,
        router_weight,
        expert_weights,
        inner_drift,
        frag_index.reshape(1, 1),
        out_grad,
    )
    return pl.pallas_call(
        finish,
        out_shape=(
            jax.ShapeDtypeStruct((TOK, D), BF16),
            jax.ShapeDtypeStruct((TOK, D), BF16),
            jax.ShapeDtypeStruct((FR, HID), F32),
            jax.ShapeDtypeStruct((FR, HID), F32),
        ),
        in_specs=[vmem] * 5,
        out_specs=(anyw, anyw, anyw, anyw),
        scratch_shapes=[
            pltpu.VMEM((TOK, D), BF16),
            pltpu.VMEM((TOK, D), BF16),
            pltpu.VMEM((FR, HID), F32),
            pltpu.VMEM((FR, HID), F32),
            dma((4,)),
        ],
        compiler_params=pltpu.CompilerParams(vmem_limit_bytes=16 * 1024 * 1024),
    )(ids, rows, pseudo, outer_params, outer_momentum)


def solution(mesh):
    in_specs = (
        P(("replica", "fsdp"), None),
        P(("replica", "fsdp"), None),
        P("replica", None, None),
        P("replica", None, None, "fsdp"),
        P(None, "fsdp"),
        P(None, "fsdp"),
        P("replica", None, "fsdp"),
        P(),
        P(("replica", "fsdp"), None),
    )
    out_specs = (
        P(("replica", "fsdp"), None),
        P(("replica", "fsdp"), None),
        P(None, "fsdp"),
        P(None, "fsdp"),
    )
    return jax.shard_map(body, mesh=mesh, in_specs=in_specs, out_specs=out_specs, check_vma=False)
```

```python
import math

import jax
import jax.numpy as jnp
from jax import lax
from jax.experimental import pallas as pl
from jax.experimental.pallas import tpu as pltpu
from jax.sharding import PartitionSpec as P

D = 6144
FF = 8192
EXPERTS = 8
CAP = 3
FR = 768
TOK = 64
KC = 16
LC = D // KC
BR = CAP * KC
NX = 4
NY = 4
NZ = 2
HID = 128
ROWS = 96
QR = FR // 4
HR = QR // 2

inner_rate = 2.0
outer_rate = 0.7
momentum_decay = 0.9
scale_in = 1.0 / math.sqrt(D)
scale_hid = 1.0 / math.sqrt(FF)

MESH = pl.DeviceIdType.MESH
F32 = jnp.float32
BF16 = jnp.bfloat16
NT = (((1,), (1,)), ((), ()))
TN = (((0,), (0,)), ((), ()))


def dot(a, b, dims=(((1,), (0,)), ((), ()))):
    return lax.dot_general(a, b, dims, preferred_element_type=F32)


def iota(shape, dim):
    return lax.broadcasted_iota(jnp.int32, shape, dim)


def one(mask):
    return jnp.where(mask, 1.0, 0.0)


POS = (0, 1, 3, 2)
GROUP = ((0, 1), (1, 2), (3, 1))
MEMBERS = ((0,), (1, 3), (2,))


def row(slab, z, p):
    return ((slab * NZ + z) * 4 + POS[p]) * BR


def group_rows(slab, z, g):
    return pl.ds(((slab * NZ + z) * 4 + GROUP[g][0]) * BR, GROUP[g][1] * BR)


def id_rows(ids):
    id0, id1 = ids[0:1, :], ids[1:2, :]
    at = iota((16, TOK), 0)
    routed = one((id0 == 0) | (id1 == 0))
    other = (id0 + id1).astype(F32)
    return jnp.where(at == 0, routed, jnp.where(at == 1, other, 0.0)).astype(BF16)


def kernel(
    tokens,
    ids_hbm,
    router_hbm,
    weights,
    drift,
    frag_hbm,
    grads,
    out_rows,
    out_pseudo,
    ids,
    router,
    frag,
    tokv,
    grdv,
    wgu,
    wdn,
    drfv,
    perm,
    ag,
    xv,
    gv,
    yv,
    rb,
    t2,
    d2,
    e1,
    fq,
    fb,
    fs,
    fh,
    fr,
    ps,
    load_sem,
    n_send,
    n_recv,
    r_send,
    r_recv,
    w_send,
    w_recv,
    t2_send,
    t2_recv,
    d2_send,
    d2_recv,
    e1_send,
    e1_recv,
    f_send,
    f_recv,
    q_send,
    q_recv,
    p_send,
    p_recv,
):
    rep = lax.axis_index("replica")
    me = lax.axis_index("fsdp")
    core = me % 2
    py = (me // 2) % NY
    px = (me // (2 * NY)) % NX
    pz = me // (2 * NY * NX)
    first = 1 - core

    def dev(z, x, y, c):
        return {"fsdp": ((z * NX + x) * NY + y) * 2 + c}

    def at1(z, step):
        x = (px + first * step) % NX
        y = (py + core * step) % NY
        return dev((pz + z) % NZ, x, y, core)

    def at2(step):
        return dev(pz, (px + core * step) % NX, (py + first * step) % NY, core)

    up2, dn2 = at2(1), at2(3)
    sib = dev(pz, px, py, 1 - core)
    near = {(z, p): at1(z, p) for z in range(NZ) for p in range(4) if (z, p) != (0, 0)}
    reps = [{"replica": (rep + d) % 4} for d in (1, 2, 3)]

    def load(src, dst, i):
        c = pltpu.make_async_copy(src, dst, load_sem.at[i])
        c.start()
        return c

    load_ids = load(ids_hbm, ids, 6)
    load_rtr = load(router_hbm, router, 7)
    load_frag = load(frag_hbm, frag, 8)
    load_tok = load(tokens, tokv, 0)
    load_grd = load(grads, grdv, 1)

    barrier = pltpu.get_barrier_semaphore()
    peers = [up2, dn2, sib] + list(near.values()) + reps
    for p in peers:
        pl.semaphore_signal(barrier, inc=1, device_id=p, device_id_type=MESH)

    def send(src, dst, ssem, rsem, to):
        c = pltpu.make_async_remote_copy(
            src_ref=src, dst_ref=dst, send_sem=ssem, recv_sem=rsem,
            device_id=to, device_id_type=MESH,
        )
        c.start()
        return c

    def arrived(dst, rsem):
        pltpu.make_async_copy(dst, dst, rsem).wait()

    pending = []

    load_ids.wait()
    rows8 = id_rows(ids)
    wide = (TOK, KC * TOK)
    tiled = dot(rows8, one(iota(wide, 0) == iota(wide, 1) % TOK).astype(BF16))
    count = dot(rows8, one(iota(wide, 0) <= iota(wide, 1) % TOK).astype(BF16))
    sshape = (BR, KC * TOK)
    smask = (
        (tiled[0:1] > 0.5)
        & (count[0:1] - 1.0 == (iota(sshape, 0) // KC).astype(F32))
        & (iota(sshape, 0) % KC == iota(sshape, 1) // TOK)
    )
    select = one(smask).astype(BF16)
    def fold(ref):
        stacked = jnp.concatenate([ref[:, k * LC : (k + 1) * LC] for k in range(KC)], axis=0)
        return dot(select, stacked)

    load_tok.wait()
    xsel = fold(tokv)
    ag[0, 0:BR, :] = xsel.astype(BF16)

    pl.semaphore_wait(barrier, len(peers))

    def piece(ref, i, slab, z, p):
        return ref.at[i, pl.ds(row(slab, z, p), BR), :]

    def group(ref, i, slab, z, g):
        return ref.at[i, group_rows(slab, z, g), :]

    def put(src, dst, ssem, rsem, to):
        pending.append(send(src, dst, ssem, rsem, to))

    far_last = [(1, 0), (0, 1), (0, 3), (1, 1), (1, 3), (0, 2), (1, 2)]

    def to_near(i):
        for z, p in far_last:
            q = (4 - p) % 4
            put(
                piece(ag, i, 0, 0, 0), piece(ag, i, 0, z, q),
                n_send.at[i, z * 4 + p], n_recv.at[i, z * 4 + q], near[z, p],
            )

    def to_ring(i, z, g):
        j = z * 3 + g
        src = group(ag, i, 0, z, g)
        put(src, group(ag, i, 3, z, g), r_send.at[i, 0, j], r_recv.at[i, 3, j], up2)
        put(src, group(ag, i, 1, z, g), r_send.at[i, 1, j], r_recv.at[i, 1, j], dn2)

    def near_to_ring(i, z, g):
        for p in MEMBERS[g]:
            arrived(piece(ag, i, 0, z, p), n_recv.at[i, z * 4 + p])
        to_ring(i, z, g)

    def got_ring(i, slab, z, g):
        arrived(group(ag, i, slab, z, g), r_recv.at[i, slab, z * 3 + g])

    def relay(i, z, g):
        j = z * 3 + g
        got_ring(i, 3, z, g)
        if z == 0:
            src = group(ag, i, 3, z, g)
            put(src, group(ag, i, 2, z, g), r_send.at[i, 2, j], r_recv.at[i, 2, j], up2)
        got_ring(i, 1, z, g)
        if z == 1:
            src = group(ag, i, 1, z, g)
            put(src, group(ag, i, 2, z, g), r_send.at[i, 2, j], r_recv.at[i, 2, j], dn2)

    def unfold(i, dst, lo, hi):
        @pl.loop(lo, hi, unroll=True)
        def _(g):
            rows_at = pl.ds(pl.multiple_of(g * 16, 16), 16)
            v = ag[i, pl.ds(pl.multiple_of(g * 256, 256), 256), :]
            r = dot(perm[...], v).astype(BF16)
            for k in range(KC):
                dst[rows_at, k * LC : (k + 1) * LC] = r[16 * k : 16 * k + 16]

    to_ring(0, 0, 0)
    to_near(0)

    other48 = jnp.sum(jnp.where(smask, tiled[1:2], 0.0), axis=1, keepdims=True)
    dshape = (BR, KC * EXPERTS)
    expert = iota(dshape, 1) % EXPERTS
    signs = jnp.where(
        iota(dshape, 0) % KC == iota(dshape, 1) // EXPERTS,
        one(expert == 0) - one(expert.astype(F32) == other48),
        0.0,
    ).astype(BF16)
    load_rtr.wait()
    load_frag.wait()
    rw = router[0].astype(F32)
    router2 = jnp.concatenate([rw[:, k * LC : (k + 1) * LC] for k in range(KC)], axis=0)
    differ = dot(signs, router2.astype(BF16))

    pshape = (256, 256)
    perm[...] = one(
        (iota(pshape, 0) // 16 == iota(pshape, 1) % 16)
        & (iota(pshape, 0) % 16 == iota(pshape, 1) // 16)
    ).astype(BF16)
    logit = jnp.sum((xsel * differ).reshape(CAP, KC, LC), axis=(1, 2), keepdims=True)
    prob = jax.nn.sigmoid(jnp.broadcast_to(logit * scale_in, (CAP, KC, LC)).reshape(BR, LC))
    load_grd.wait()
    gsel = fold(grdv)
    ag[1, 0:BR, :] = (prob * gsel).astype(BF16)
    to_ring(1, 0, 0)
    to_near(1)

    loads = []
    for m, (dst, lo, far) in enumerate(((wgu, 0, 2 * HID), (wgu, HID, 3 * HID), (wdn, 0, HID))):
        src = weights.at[0, m]
        loads.append(load(src, dst.at[:, lo : lo + HID], 2 + m))
        put(src, dst.at[:, far : far + HID], w_send.at[m], w_recv.at[m], sib)
    loads.append(load(drift.at[0], drfv, 5))

    order = [(0, 0), (1, 0), (0, 1), (1, 1), (0, 2), (1, 2)]
    for j in range(1, 10):
        if j < 6:
            near_to_ring(0, *order[j])
        if j > 4:
            near_to_ring(1, *order[j - 4])
    for j in range(10):
        if j < 6:
            relay(0, *order[j])
        if j >= 4:
            relay(1, *order[j - 4])
    unfold(0, xv, 0, 3)
    unfold(1, gv, 0, 3)
    for z, g in order:
        got_ring(0, 2, z, g)
    unfold(0, xv, 3, 6)

    for c in loads:
        c.wait()
    for m, (dst, far) in enumerate(((wgu, 2 * HID), (wgu, 3 * HID), (wdn, HID))):
        arrived(dst.at[:, far : far + HID], w_recv.at[m])
    gu = dot(xv[...], wgu[...]) * scale_in
    gate = jnp.concatenate([gu[:, 0:HID], gu[:, 2 * HID : 3 * HID]], axis=1)
    up = jnp.concatenate([gu[:, HID : 2 * HID], gu[:, 3 * HID :]], axis=1)
    sigma = jax.nn.sigmoid(gate)
    active = gate * sigma
    hidden = (active * up).astype(BF16)
    def back(i, rows_at, w, scale):
        for k in range(KC):
            part = dot(rows_at, w[k * LC : (k + 1) * LC, :], NT)
            for c in range(LC // 128):
                lanes = slice(c * 128, (c + 1) * 128)
                yv[i, c, pl.ds(k, ROWS, stride=KC), :] = part[:, lanes] * scale

    def refold(i, lo, hi):
        at = pl.ds(lo * 256, (hi - lo) * 256)
        for c in range(LC // 128):
            rb[i, at, c * 128 : (c + 1) * 128] = yv[i, c, at, :].astype(BF16)

    def transit(i, way, g):
        at = pl.ds(GROUP[g][0] * BR, GROUP[g][1] * BR)
        return t2.at[i, way, at, :]

    def landing(i, way, z, g):
        return d2.at[i, way, group_rows(0, z, g), :]

    def send_transit(i, way, g, to):
        put(
            group(rb, i, 2, way, g), transit(i, way, g),
            t2_send.at[i, way, g], t2_recv.at[i, way, g], to,
        )

    def send_landing(i, way, slab, z, g, to):
        j = z * 3 + g
        put(
            group(rb, i, slab, z, g), landing(i, way, z, g),
            d2_send.at[i, way, j], d2_recv.at[i, way, j], to,
        )

    def add_into(i, at, *others):
        v = rb[i, at, :].astype(F32)
        for other in others:
            v = v + other[...].astype(F32)
        rb[i, at, :] = v.astype(BF16)

    def scatter_start(i):
        refold(i, 3, 6)
        for g in (2, 1, 0):
            send_transit(i, 0, g, up2)
            send_transit(i, 1, g, dn2)
        refold(i, 0, 3)

    def scatter_direct(i, g):
        send_landing(i, 0, 1, 1, g, up2)
        send_landing(i, 1, 3, 0, g, dn2)

    def scatter_relay(i, g):
        arrived(transit(i, 0, g), t2_recv.at[i, 0, g])
        add_into(i, group_rows(1, 0, g), transit(i, 0, g))
        send_landing(i, 0, 1, 0, g, up2)
        arrived(transit(i, 1, g), t2_recv.at[i, 1, g])
        add_into(i, group_rows(3, 1, g), transit(i, 1, g))
        send_landing(i, 1, 3, 1, g, dn2)

    def scatter_near(i, g):
        for z in (1, 0):
            for way in range(2):
                arrived(landing(i, way, z, g), d2_recv.at[i, way, z * 3 + g])
            add_into(i, group_rows(0, z, g), landing(i, 0, z, g), landing(i, 1, z, g))
            for p in MEMBERS[g]:
                if (z, p) != (0, 0):
                    j = z * 4 + (4 - p) % 4
                    put(
                        piece(rb, i, 0, z, p), e1.at[i, j],
                        e1_send.at[i, z * 4 + p], e1_recv.at[i, j], near[z, p],
                    )

    def scatter_end(i):
        v = rb[i, 0:BR, :].astype(F32)
        for z, p in far_last:
            j = z * 4 + p
            arrived(e1.at[i, j], e1_recv.at[i, j])
            v = v + e1[i, j].astype(F32)
        return v

    back(0, hidden, wdn, scale_hid)
    scatter_start(0)
    for g in (2, 1, 0):
        scatter_direct(0, g)
    for z, g in order:
        got_ring(1, 2, z, g)
    unfold(1, gv, 3, 6)
    d_hidden = dot(gv[...], wdn[...]) * scale_hid
    d_gate = (d_hidden * up * (sigma + gate * sigma * (1.0 - sigma))).astype(BF16)
    d_up = (d_hidden * active).astype(BF16)
    d_gu = jnp.concatenate(
        [d_gate[:, :HID], d_up[:, :HID], d_gate[:, HID:], d_up[:, HID:]], axis=1
    )

    which = frag[...]
    per = D // FR
    masks = [one((which >= m * per) & (which < (m + 1) * per)) for m in range(3)]
    left = jnp.zeros((ROWS, FR), BF16)
    for src, off in ((xv, 1.0 - masks[2]), (gv, masks[2])):
        for c in range(per):
            here = one((which == c) | (which == per + c) | (which == 2 * per + c))
            left = left + src[:, c * FR : (c + 1) * FR] * (off * here).astype(BF16)
    right = (
        d_gate * masks[0].astype(BF16)
        + d_up * masks[1].astype(BF16)
        + hidden * masks[2].astype(BF16)
    )
    factor = inner_rate * (scale_in * (1.0 - masks[2]) + scale_hid * masks[2])
    partial = dot(left, right, TN) * factor
    fb[...] = partial[:, HID:].astype(BF16)
    put(fb, fs, f_send, f_recv, sib)
    fq[...] = partial[:, :HID] - drfv[...]

    back(1, d_gu, wgu, scale_in)
    scatter_start(1)
    scatter_relay(0, 2)
    scatter_relay(0, 1)
    scatter_relay(0, 0)
    arrived(fs, f_recv)
    fq[...] = fq[...] + fs[...].astype(F32)
    fh[...] = fq[...].astype(BF16)

    def half(quarter, h):
        return pl.ds(pl.multiple_of(quarter * QR + h * HR, 32), HR)

    for h in range(2):
        for d in (1, 0, 2):
            at = half((rep + d + 1) % 4, h)
            put(fh.at[at, :], fr.at[d, h], q_send.at[d, h], q_recv.at[d, h], reps[d])

    def sum_quarter(h):
        own = half(rep, h)
        total = fq[own, :]
        for d in range(3):
            arrived(fr.at[d, h], q_recv.at[d, h])
            total = total + fr[d, h].astype(F32)
        ps[own, :] = (total * 0.25).astype(BF16)
        for d in (1, 0, 2):
            put(ps.at[own, :], ps.at[own, :], p_send.at[d, h], p_recv.at[d, h], reps[d])

    scatter_direct(1, 2)
    scatter_direct(1, 1)
    scatter_relay(1, 2)
    scatter_near(0, 2)
    scatter_direct(1, 0)
    scatter_relay(1, 1)
    scatter_near(0, 1)
    scatter_relay(1, 0)
    scatter_near(0, 0)
    sum_quarter(0)
    sum_quarter(1)
    scatter_near(1, 2)
    scatter_near(1, 1)
    scatter_near(1, 0)
    y = scatter_end(0)

    d_prob = jnp.sum((gsel * y).reshape(CAP, KC, LC), axis=(1, 2), keepdims=True)
    d_prob = jnp.broadcast_to(d_prob, (CAP, KC, LC)).reshape(BR, LC)
    d_logit = d_prob * prob * (1.0 - prob)
    out_rows[0] = (prob * y).astype(BF16)
    dx = scatter_end(1)
    out_rows[1] = (dx + (d_logit * scale_in) * differ).astype(BF16)

    for h in range(2):
        for d in range(3):
            at = half((rep + 3 - d) % 4, h)
            arrived(ps.at[at, :], p_recv.at[d, h])
    out_pseudo[...] = ps[...]

    for c in pending:
        c.wait_send()


def finish(
    ids, rows, pseudo, params, momentum,
    out_mixed, out_grad, out_params, out_momentum,
    mixv, grdv, parv, momv, sem,
):
    def store(src, dst, i):
        c = pltpu.make_async_copy(src, dst, sem.at[i])
        c.start()
        return c


    rows8 = id_rows(ids)
    tri = one(iota((TOK, TOK), 0) >= iota((TOK, TOK), 1)).astype(BF16)
    eye = one(iota((TOK, TOK), 0) == iota((TOK, TOK), 1)).astype(BF16)
    slot = dot(tri, rows8, NT)[:, 0:1] - 1.0
    routed = dot(eye, rows8, NT)[:, 0:1]
    shape = (TOK, BR)
    mine = (slot == (iota(shape, 1) // KC).astype(F32)) & (routed > 0.5)
    spread = jnp.concatenate(
        [one(mine & (iota(shape, 1) % KC == k)).astype(BF16) for k in range(KC)], axis=0
    )
    stores = []
    for src, buf, dst in ((0, mixv, out_mixed), (1, grdv, out_grad)):
        placed = dot(spread, rows[src]).astype(BF16)
        for k in range(KC):
            buf[:, k * LC : (k + 1) * LC] = placed[k * TOK : (k + 1) * TOK]
        stores.append(store(buf, dst, 2 + src))
    shift = pseudo[...].astype(F32)
    mom = momentum_decay * momentum[...] + shift
    momv[...] = mom
    stores.append(store(momv, out_momentum, 0))
    parv[...] = params[...] - outer_rate * (shift + momentum_decay * mom)
    stores.append(store(parv, out_params, 1))
    for c in stores:
        c.wait()


def body(
    tokens,
    expert_ids,
    router_weight,
    expert_weights,
    outer_params,
    outer_momentum,
    inner_drift,
    frag_index,
    out_grad,
):
    vmem = pl.BlockSpec(memory_space=pltpu.VMEM)
    anyw = pl.BlockSpec(memory_space=pl.ANY)
    dma = pltpu.SemaphoreType.DMA
    scratch = [
        pltpu.VMEM((2, TOK), jnp.int32),
        pltpu.VMEM((1, EXPERTS, D), BF16),
        pltpu.VMEM((1, 1), jnp.int32),
        pltpu.VMEM((TOK, D), BF16),
        pltpu.VMEM((TOK, D), BF16),
        pltpu.VMEM((D, 4 * HID), BF16),
        pltpu.VMEM((D, 2 * HID), BF16),
        pltpu.VMEM((FR, HID), F32),
        pltpu.VMEM((256, 256), BF16),
        pltpu.VMEM((2, ROWS * KC, LC), BF16),
        pltpu.VMEM((ROWS, D), BF16),
        pltpu.VMEM((ROWS, D), BF16),
        pltpu.VMEM((2, LC // 128, ROWS * KC, 128), F32),
        pltpu.VMEM((2, ROWS * KC, LC), BF16),
        pltpu.VMEM((2, 2, 4 * BR, LC), BF16),
        pltpu.VMEM((2, 2, 8 * BR, LC), BF16),
        pltpu.VMEM((2, 8, BR, LC), BF16),
        pltpu.VMEM((FR, HID), F32),
        pltpu.VMEM((FR, HID), BF16),
        pltpu.VMEM((FR, HID), BF16),
        pltpu.VMEM((FR, HID), BF16),
        pltpu.VMEM((3, 2, HR, HID), BF16),
        pltpu.VMEM((FR, HID), BF16),
        dma((9,)),
        dma((2, 8)),
        dma((2, 8)),
        dma((2, 3, 6)),
        dma((2, 4, 6)),
        dma((3,)),
        dma((3,)),
        dma((2, 2, 3)),
        dma((2, 2, 3)),
        dma((2, 2, 6)),
        dma((2, 2, 6)),
        dma((2, 8)),
        dma((2, 8)),
        dma,
        dma,
        dma((3, 2)),
        dma((3, 2)),
        dma((3, 2)),
        dma((3, 2)),
    ]
    ids = expert_ids.T
    rows, pseudo = pl.pallas_call(
        kernel,
        out_shape=(
            pltpu.VMEM((2, BR, LC), BF16),
            pltpu.VMEM((FR, HID), BF16),
        ),
        in_specs=[anyw] * 7,
        out_specs=(vmem, vmem),
        scratch_shapes=scratch,
        compiler_params=pltpu.CompilerParams(
            collective_id=0, has_side_effects=True, vmem_limit_bytes=56 * 1024 * 1024
        ),
        cost_estimate=pl.CostEstimate(
            flops=4_000_000_000, bytes_accessed=12_000_000, transcendentals=100_000
        ),
    )(
        tokens,
        ids,
        router_weight,
        expert_weights,
        inner_drift,
        frag_index.reshape(1, 1),
        out_grad,
    )
    return pl.pallas_call(
        finish,
        out_shape=(
            jax.ShapeDtypeStruct((TOK, D), BF16),
            jax.ShapeDtypeStruct((TOK, D), BF16),
            jax.ShapeDtypeStruct((FR, HID), F32),
            jax.ShapeDtypeStruct((FR, HID), F32),
        ),
        in_specs=[vmem] * 5,
        out_specs=(anyw, anyw, anyw, anyw),
        scratch_shapes=[
            pltpu.VMEM((TOK, D), BF16),
            pltpu.VMEM((TOK, D), BF16),
            pltpu.VMEM((FR, HID), F32),
            pltpu.VMEM((FR, HID), F32),
            dma((4,)),
        ],
        compiler_params=pltpu.CompilerParams(vmem_limit_bytes=16 * 1024 * 1024),
    )(ids, rows, pseudo, outer_params, outer_momentum)


def solution(mesh):
    in_specs = (
        P(("replica", "fsdp"), None),
        P(("replica", "fsdp"), None),
        P("replica", None, None),
        P("replica", None, None, "fsdp"),
        P(None, "fsdp"),
        P(None, "fsdp"),
        P("replica", None, "fsdp"),
        P(),
        P(("replica", "fsdp"), None),
    )
    out_specs = (
        P(("replica", "fsdp"), None),
        P(("replica", "fsdp"), None),
        P(None, "fsdp"),
        P(None, "fsdp"),
    )
    return jax.shard_map(body, mesh=mesh, in_specs=in_specs, out_specs=out_specs, check_vma=False)
```
